256 devices in a mesh: gx: 32 (over x, y, core), gy: 8 (over z).
Axes of the slice: x: 4, y: 4, z: 8, core: 2. Of those that a mesh axis runs over, the one named last changes fastest.
Arguments:
- nodes: bfloat16 [262144, 128], P(('gx', 'gy')), may hold values from -6 to 6
- ghost_rows: int32 [256, 8, 256], P(('gx', 'gy')), may hold values from 0 to 1023
- ghost_count: int32 [256, 8], P(('gx', 'gy')), may hold values from 0 to 256, as said below
- edge_send: int32 [256, 4096], P(('gx', 'gy')), may hold values from 0 to 3071
- edge_recv: int32 [256, 4096], P(('gx', 'gy')), may hold values from 0 to 1023
- edge_count: int32 [256], P(('gx', 'gy')), may hold values from 512 to 4096, as said below
- pool_map: int32 [256, 1024], P(('gx', 'gy')), may hold values from 0 to 191, as said below
- w_edge_in: bfloat16 [256, 128], replicated, may hold values from -0.375 to 0.375
- w_edge_out: bfloat16 [128, 128], replicated, may hold values from -0.5 to 0.5
- w_node_in: bfloat16 [256, 128], replicated, may hold values from -0.375 to 0.375
- w_node_out: bfloat16 [128, 128], replicated, may hold values from -0.5 to 0.5
- w_coarse_in: bfloat16 [128, 128], replicated, may hold values from -0.5 to 0.5
- w_coarse_out: bfloat16 [128, 128], replicated, may hold values from -0.5 to 0.5
- d_fine: bfloat16 [262144, 128], P(('gx', 'gy')), may hold values from -6 to 6
- d_coarse: bfloat16 [32768, 128], P(('gx', 'gy')), may hold values from -6 to 6
Outputs:
- fine_out: bfloat16 [262144, 128], P(('gx', 'gy'))
- coarse_out: bfloat16 [32768, 128], P(('gx', 'gy'))
- grad_nodes: float32 [262144, 128], P(('gx', 'gy'))
- grad_edge_in: float32 [256, 128], replicated
- grad_edge_out: float32 [128, 128], replicated
- grad_node_in: float32 [256, 128], replicated
- grad_node_out: float32 [128, 128], replicated
- grad_coarse_in: float32 [128, 128], replicated
- grad_coarse_out: float32 [128, 128], replicated
The draws below stay inside these ranges and needn't reach their ends.
Inputs may be any that keep to these rules, and one draw needn't show every extreme that they name: `ghost_count`: every device fills all 256 slots for at least one offset. `edge_count`: at least one device has all 4096 slots live. `pool_map`: values under 32 occur only on devices that are not first along gy, and values of 160 or more only on devices that are not last along gy, so every parent lies in the device's gx column.
All inputs are finite; a program needn't handle non-finite values.
Results may differ from the reference program's by a relative error of at most 0.012.
Values may be sent and summed in bfloat16 or wider, within the bound.
No kernel may reach another device: no remote copies, remote signals or barrier semaphores. Data moves between devices by JAX's collectives and lax.ppermute only.
A program may use at most 64 MiB of HBM per device.

```python
import jax
import jax.numpy as jnp
from jax import lax

C = 128
HID = 128
GBLK = 256
BAND = 32
NODE_DEV = 1024
EDGE_DEV = 4096
CO_DEV = 128
NODES = 262144
COARSE = 32768
N_GX = 32
N_GY = 8
DEVICES = 256


def draw_ghost_count(key, part):
    key_one, key_two = jax.random.split(jax.random.fold_in(key, 11))
    counts = jax.random.randint(key_one, (N_GX * N_GY, 8), 0, GBLK + 1)
    full_peer = jax.random.randint(key_two, (N_GX * N_GY, 1), 0, 8)
    direction_ids = jnp.arange(8, dtype=jnp.int32)[None, :]
    return jnp.where(direction_ids == full_peer, GBLK, counts).astype(jnp.int32)


def draw_edge_count(key, part):
    key_one, key_two = jax.random.split(jax.random.fold_in(key, 23))
    shifts = jax.random.randint(key_one, (N_GX * N_GY,), 0, 4).astype(jnp.int32)
    counts = jnp.right_shift(jnp.full((N_GX * N_GY,), EDGE_DEV, jnp.int32), shifts)
    busiest = jax.random.randint(key_two, (), 0, N_GX * N_GY)
    device_ids = jnp.arange(N_GX * N_GY, dtype=jnp.int32)
    return jnp.where(device_ids == busiest, EDGE_DEV, counts).astype(jnp.int32)


def draw_pool_map(key, part):
    devices = N_GX * N_GY
    near = max(1, NODE_DEV // 16)
    key_one, key_two, key_three, key_four = jax.random.split(jax.random.fold_in(key, 37), 4)
    order = jax.vmap(lambda single: jax.random.permutation(single, NODE_DEV))(jax.random.split(key_one, devices))
    own_parent = jax.random.randint(key_two, (devices, NODE_DEV), BAND, BAND + CO_DEV)
    lower_parent = jax.random.randint(key_three, (devices, NODE_DEV), 0, BAND)
    upper_parent = jax.random.randint(key_four, (devices, NODE_DEV), BAND + CO_DEV, CO_DEV + 2 * BAND)
    row_idx = (jnp.arange(devices, dtype=jnp.int32) % N_GY)[:, None]
    goes_lower = (order < near) & (row_idx > 0)
    goes_upper = (order >= near) & (order < 2 * near) & (row_idx < N_GY - 1)
    return jnp.where(goes_lower, lower_parent, jnp.where(goes_upper, upper_parent, own_parent)).astype(jnp.int32)


def set_ends(drawn, own_key, low, top_value):
    longest = drawn.shape.index(max(drawn.shape))
    spots = []
    for shift in (0, 1):
        where = [jax.random.randint(jax.random.fold_in(own_key, axis), (), 0, length) for axis, length in enumerate(drawn.shape)]
        where[longest] = (where[longest] + shift) % drawn.shape[longest]
        spots.append(tuple(where))
    return drawn.at[spots[0]].set(low).at[spots[1]].set(top_value)


def level_of(key, dims, cuts, smallest, largest):
    def one(axis_at, blocks):
        draws = jax.random.uniform(jax.random.fold_in(jax.random.fold_in(key, 6), axis_at), (blocks,), jnp.float32, smallest / len(cuts), largest / len(cuts))
        return jnp.repeat(jnp.exp(draws), dims[axis_at] // blocks).reshape((-1,) + (1,) * (len(dims) - axis_at - 1))

    loudness = one(*cuts[0])
    for cut in cuts[1:]:
        loudness = loudness * one(*cut)
    return loudness


def normal_values(rng, dims, scale, reach, shards=(), kind=jnp.bfloat16):
    gain = level_of(rng, dims, shards, -0.22, 0.18) if shards else 1.0
    entries = jax.random.normal(rng, dims, jnp.float32) * scale * gain
    return jnp.minimum(jnp.maximum(entries, -reach), reach).astype(kind)


def setup_inputs(seed: int = 0) -> dict:
    splits = jax.random.split(jax.random.key(seed), 16)
    return {
        "nodes": normal_values(splits[0], (NODES, C), 1.0, 6.0, ((0, 256),)),
        "ghost_rows": set_ends(jax.random.randint(splits[1], (DEVICES, 8, GBLK), 0, NODE_DEV), jax.random.fold_in(splits[1], 1), 0, NODE_DEV - 1).astype(jnp.int32),
        "ghost_count": draw_ghost_count(jax.random.fold_in(splits[15], 71), 0),
        "edge_send": set_ends(jax.random.randint(splits[3], (DEVICES, EDGE_DEV), 0, NODE_DEV + 8 * GBLK), jax.random.fold_in(splits[3], 1), 0, (NODE_DEV + 8 * GBLK) - 1).astype(jnp.int32),
        "edge_recv": set_ends(jax.random.randint(splits[4], (DEVICES, EDGE_DEV), 0, NODE_DEV), jax.random.fold_in(splits[4], 1), 0, NODE_DEV - 1).astype(jnp.int32),
        "edge_count": draw_edge_count(jax.random.fold_in(splits[15], 71), 0),
        "pool_map": draw_pool_map(jax.random.fold_in(splits[15], 71), 0),
        "w_edge_in": normal_values(splits[7], (2 * C, HID), (2 * C) ** -0.5, 0.375),
        "w_edge_out": normal_values(splits[8], (HID, C), HID ** -0.5, 0.5),
        "w_node_in": normal_values(splits[9], (2 * C, HID), (2 * C) ** -0.5, 0.375),
        "w_node_out": normal_values(splits[10], (HID, C), HID ** -0.5, 0.5),
        "w_coarse_in": normal_values(splits[11], (C, HID), C ** -0.5, 0.5),
        "w_coarse_out": normal_values(splits[12], (HID, C), HID ** -0.5, 0.5),
        "d_fine": normal_values(splits[13], (NODES, C), 1.0, 6.0, ((0, 256),)),
        "d_coarse": normal_values(splits[14], (COARSE, C), 1.0, 6.0, ((0, 256),)),
    }


offset_across = (-1, -1, -1, 0, 0, 1, 1, 1)
offset_along = (-1, 0, 1, -1, 1, -1, 0, 1)


def matmul(left, right):
    return jnp.dot(left, right, preferred_element_type=jnp.float32)


def silu_slope(pre_value):
    sigmoid_v = jax.nn.sigmoid(pre_value)
    return sigmoid_v * (1.0 + pre_value * (1.0 - sigmoid_v))


def fine_forward(owned, ghosts, send_index, recv_index, edge_live, weights):
    w_edge_in, w_edge_out, w_node_in, w_node_out = weights
    latent = owned.shape[1]
    lookup = jnp.concatenate([owned, ghosts], axis=0)
    senders = lookup[send_index]
    receivers = owned[recv_index]
    edge_pre = matmul(senders, w_edge_in[:latent]) + matmul(receivers, w_edge_in[latent:])
    edge_act = jax.nn.silu(edge_pre).astype(jnp.bfloat16)
    message = (matmul(edge_act, w_edge_out) * edge_live[:, None]).astype(jnp.bfloat16)
    summed = jax.ops.segment_sum(message.astype(jnp.float32), recv_index, num_segments=owned.shape[0]).astype(jnp.bfloat16)
    node_pre = matmul(owned, w_node_in[:latent]) + matmul(summed, w_node_in[latent:])
    node_act = jax.nn.silu(node_pre).astype(jnp.bfloat16)
    fine_out = (owned.astype(jnp.float32) + matmul(node_act, w_node_out)).astype(jnp.bfloat16)
    return fine_out, (senders, receivers, edge_pre, edge_act, summed, node_pre, node_act)


def fine_backward(owned, send_index, recv_index, edge_live, weights, stashed, d_total, lookup_rows):
    w_edge_in, w_edge_out, w_node_in, w_node_out = weights
    senders, receivers, edge_pre, edge_act, summed, node_pre, node_act = stashed
    rows_here, latent = owned.shape
    d_out16 = d_total.astype(jnp.bfloat16)
    g_node_out = matmul(node_act.T, d_out16)
    d_node_pre = (matmul(d_out16, w_node_out.T) * silu_slope(node_pre)).astype(jnp.bfloat16)
    g_node_in = jnp.concatenate([matmul(owned.T, d_node_pre), matmul(summed.T, d_node_pre)], axis=0)
    d_owned = d_total + matmul(d_node_pre, w_node_in[:latent].T)
    d_summed = matmul(d_node_pre, w_node_in[latent:].T).astype(jnp.bfloat16)
    d_message = d_summed[recv_index] * edge_live[:, None].astype(d_summed.dtype)
    g_edge_out = matmul(edge_act.T, d_message)
    d_edge_pre = (matmul(d_message, w_edge_out.T) * silu_slope(edge_pre)).astype(jnp.bfloat16)
    g_edge_in = jnp.concatenate([matmul(senders.T, d_edge_pre), matmul(receivers.T, d_edge_pre)], axis=0)
    d_senders = matmul(d_edge_pre, w_edge_in[:latent].T)
    d_receivers = matmul(d_edge_pre, w_edge_in[latent:].T)
    d_lookup = jax.ops.segment_sum(d_senders, send_index, num_segments=lookup_rows)
    d_owned = d_owned + d_lookup[:rows_here] + jax.ops.segment_sum(d_receivers, recv_index, num_segments=rows_here)
    return d_owned, d_lookup[rows_here:], (g_edge_in, g_edge_out, g_node_in, g_node_out)


def reference(nodes, ghost_rows, ghost_count, edge_send, edge_recv, edge_count, pool_map, w_edge_in, w_edge_out, w_node_in, w_node_out, w_coarse_in, w_coarse_out, d_fine, d_coarse):
    devices = N_GX * N_GY
    latent = nodes.shape[1]
    per_device = nodes.reshape(devices, NODE_DEV, latent)
    d_fine_dev = d_fine.reshape(devices, NODE_DEV, latent)
    weights = (w_edge_in, w_edge_out, w_node_in, w_node_out)
    slot_ids = jnp.arange(GBLK, dtype=jnp.int32)
    edge_ids = jnp.arange(EDGE_DEV, dtype=jnp.int32)
    column_ids = jnp.arange(N_GX, dtype=jnp.int32)
    device_ids = jnp.arange(devices, dtype=jnp.int32)
    direction_ids = jnp.arange(8, dtype=jnp.int32)
    across = jnp.array(offset_across, dtype=jnp.int32)
    along = jnp.array(offset_along, dtype=jnp.int32)

    def halo_of(device):
        column_idx = device // N_GY
        row_idx = device % N_GY
        source_column = column_idx - across
        source_row = row_idx - along
        inside = (source_column >= 0) & (source_column < N_GX) & (source_row >= 0) & (source_row < N_GY)
        sources = jnp.clip(source_column, 0, N_GX - 1) * N_GY + jnp.clip(source_row, 0, N_GY - 1)
        ghost_lists = ghost_rows[sources, direction_ids]
        slot_live = (slot_ids[None, :] < ghost_count[sources, direction_ids][:, None]) & inside[:, None]
        picked = per_device[sources[:, None], ghost_lists]
        picked = jnp.where(slot_live[:, :, None], picked, jnp.zeros_like(picked))
        return picked, sources, ghost_lists, slot_live

    def forward_of(device):
        picked, sources, ghost_lists, slot_live = halo_of(device)
        edge_live = (edge_ids < edge_count[device]).astype(jnp.float32)
        return fine_forward(per_device[device], picked.reshape(8 * GBLK, latent), edge_send[device], edge_recv[device], edge_live, weights), edge_live, sources, ghost_lists, slot_live

    fine_all = lax.map(lambda device: forward_of(device)[0][0], device_ids)
    column_rows = N_GY * CO_DEV

    def parents_of(device):
        return pool_map[device] + (device % N_GY) * CO_DEV - BAND

    def pool_column(column_idx):
        members = column_idx * N_GY + jnp.arange(N_GY, dtype=jnp.int32)

        def one_member(values, member):
            return jax.ops.segment_sum(values.astype(jnp.float32), parents_of(member), num_segments=column_rows)

        parts = jax.vmap(one_member)(fine_all[members], members)
        return (0.125 * jnp.sum(parts, axis=0)).astype(jnp.bfloat16)

    coarse_in = lax.map(pool_column, column_ids).reshape(N_GX * column_rows, latent)
    coarse_pre = matmul(coarse_in, w_coarse_in)
    coarse_act = jax.nn.silu(coarse_pre).astype(jnp.bfloat16)
    coarse_out = (coarse_in.astype(jnp.float32) + matmul(coarse_act, w_coarse_out)).astype(jnp.bfloat16)
    g_coarse_out = matmul(coarse_act.T, d_coarse)
    d_coarse_pre = (matmul(d_coarse, w_coarse_out.T) * silu_slope(coarse_pre)).astype(jnp.bfloat16)
    g_coarse_in = matmul(coarse_in.T, d_coarse_pre)
    d_coarse_in = (d_coarse.astype(jnp.float32) + matmul(d_coarse_pre, w_coarse_in.T)).astype(jnp.bfloat16)
    d_column = d_coarse_in.reshape(N_GX, column_rows, latent)

    def backward_step(carry, device):
        grads_nodes, totals = carry
        outcome, edge_live, sources, ghost_lists, slot_live = forward_of(device)
        stashed = outcome[1]
        column_idx = device // N_GY
        d_total = d_fine_dev[device].astype(jnp.float32) + 0.125 * d_column[column_idx][parents_of(device)].astype(jnp.float32)
        d_owned, d_ghosts, partials = fine_backward(per_device[device], edge_send[device], edge_recv[device], edge_live, weights, stashed, d_total, NODE_DEV + 8 * GBLK)
        rounded = lax.optimization_barrier(d_ghosts.astype(jnp.bfloat16)).astype(jnp.float32).reshape(8, GBLK, latent)
        rounded = jnp.where(slot_live[:, :, None], rounded, jnp.zeros_like(rounded))
        grads_nodes = grads_nodes.at[device].add(d_owned)
        grads_nodes = grads_nodes.at[sources[:, None], ghost_lists].add(rounded)
        totals = tuple(total + term for total, term in zip(totals, partials))
        return (grads_nodes, totals), None

    start_totals = (jnp.zeros((2 * latent, HID), jnp.float32), jnp.zeros((HID, latent), jnp.float32), jnp.zeros((2 * latent, HID), jnp.float32), jnp.zeros((HID, latent), jnp.float32))
    start_grads = jnp.zeros((devices, NODE_DEV, latent), jnp.float32)
    (grads_nodes, totals), unused = lax.scan(backward_step, (start_grads, start_totals), device_ids)
    grad_scale = 1.0 / (NODE_DEV * devices) ** 0.5
    return (fine_all.reshape(devices * NODE_DEV, latent), coarse_out, grads_nodes.reshape(devices * NODE_DEV, latent), totals[0] * grad_scale, totals[1] * grad_scale, totals[2] * grad_scale, totals[3] * grad_scale, g_coarse_in * grad_scale, g_coarse_out * grad_scale)
```

```python
import jax
import jax.numpy as jnp
from jax import lax
from jax.experimental import pallas as pl
from jax.experimental.pallas import tpu as pltpu
from jax.sharding import Mesh
from jax.sharding import PartitionSpec as P

BAND = 32
LAT = 128
LOW = 512
BITS = 9
STEP = 512
GX_GY = ("gx_0", "gx_1", "gx_2", "gy")
GX = ("gx_0", "gx_1", "gx_2")
MIB = 1024 * 1024

f32 = jnp.float32
bf16 = jnp.bfloat16


def mm(left, right):
    return jnp.dot(left, right, preferred_element_type=f32)


def mm_nt(left, right):
    return lax.dot_general(left, right, (((1,), (1,)), ((), ())), preferred_element_type=f32)


def mm_tn(left, right):
    return lax.dot_general(left, right, (((0,), (0,)), ((), ())), preferred_element_type=f32)


def wide(table):
    groups = table.shape[0] // LOW
    return jnp.concatenate([table[i * LOW : (i + 1) * LOW] for i in range(groups)], axis=1)


def tall(table):
    groups = table.shape[1] // LAT
    return jnp.concatenate([table[:, i * LAT : (i + 1) * LAT] for i in range(groups)], axis=0)


def in_columns(row):
    parts = []
    for j in range(row.shape[1] // LAT):
        parts.append(jnp.broadcast_to(row[:, j * LAT : (j + 1) * LAT], (LAT, LAT)).T)
    return jnp.concatenate(parts, axis=0)


def one_hot(col, rows):
    lanes = lax.broadcasted_iota(jnp.int32, col.shape, 1)
    return jnp.concatenate(
        [(col == lanes + j * LAT).astype(f32).astype(bf16) for j in range(rows // LAT)], axis=1
    )


def one_hot_t(row, rows):
    ids = lax.broadcasted_iota(jnp.int32, (rows, row.shape[1]), 0)
    return (ids == row).astype(f32).astype(bf16)


def take(col, table):
    got = mm(one_hot(col & (LOW - 1), LOW), table)
    group = col >> BITS
    total = jnp.zeros((col.shape[0], LAT), f32)
    for i in range(table.shape[1] // LAT):
        total = jnp.where(group == i, got[:, i * LAT : (i + 1) * LAT], total)
    return total


def put(row, col, values, groups):
    group = col >> BITS
    spread = jnp.concatenate(
        [jnp.where(group == i, values, 0.0).astype(bf16) for i in range(groups)], axis=1
    )
    return mm(one_hot_t(row & (LOW - 1), LOW), spread)


def sigmoid(v):
    return 1.0 / (1.0 + jnp.exp(-v))


def act_and_slope(v):
    s = sigmoid(v)
    return v * s, s * (1.0 + v * (1.0 - s))


def live_row(row, first, count):
    ids = lax.broadcasted_iota(jnp.int32, row.shape, 1) + first
    return jnp.where(ids < count, row, -1)


def pick_kernel(count_ref, rows_ref, nodes_ref, up_ref, down_ref, mid_ref):
    table = wide(nodes_ref[...])
    slots = rows_ref.shape[2]
    for k in range(8):
        row = live_row(rows_ref[0, k : k + 1, :], 0, count_ref[0, k])
        got = take(in_columns(row), table).astype(bf16)
        if k < 3:
            down_ref[k * slots : (k + 1) * slots, :] = got
        elif k < 5:
            mid_ref[(k - 3) * slots : (k - 2) * slots, :] = got
        else:
            up_ref[(k - 5) * slots : (k - 4) * slots, :] = got


def own_kernel(count_ref, send_ref, recv_ref, nodes_ref, sown_ref, recvs_ref, table):
    step = pl.program_id(0)

    @pl.when(step == 0)
    def _():
        table[...] = wide(nodes_ref[...])

    first = step * STEP
    count = count_ref[0]
    sown_ref[...] = take(in_columns(live_row(send_ref[...], first, count)), table[...]).astype(bf16)
    recvs_ref[...] = take(in_columns(live_row(recv_ref[...], first, count)), table[...]).astype(bf16)


def forward_kernel(
    count_ref,
    send_ref,
    recv_ref,
    sown_ref,
    recvs_ref,
    up_ref,
    down_ref,
    yup_ref,
    ydown_ref,
    nodes_ref,
    pool_ref,
    wei_ref,
    weo_ref,
    wni_ref,
    wno_ref,
    senders_ref,
    act_ref,
    slope_ref,
    fine_ref,
    summed_ref,
    nact_ref,
    nslope_ref,
    window_ref,
    wlow_ref,
    whigh_ref,
    table,
    acc,
):
    step = pl.program_id(0)
    slots = up_ref.shape[0] // 3

    @pl.when(step == 0)
    def _():
        def block(ref, i):
            return ref[i * slots : (i + 1) * slots, :]

        blocks = (
            block(ydown_ref, 2),
            block(down_ref, 1),
            block(yup_ref, 2),
            block(ydown_ref, 1),
            block(yup_ref, 1),
            block(ydown_ref, 0),
            block(up_ref, 1),
            block(yup_ref, 0),
        )
        for k in range(8):
            table[(k % 2) * slots : (k % 2 + 1) * slots, (k // 2) * LAT : (k // 2 + 1) * LAT] = blocks[k]
        acc[...] = jnp.zeros_like(acc)

    first = step * STEP
    count = count_ref[0]
    owned = nodes_ref.shape[0]
    send = in_columns(live_row(send_ref[...], first, count)) - owned
    senders = (take(send, table[...]) + sown_ref[...].astype(f32)).astype(bf16)
    senders_ref[...] = senders
    pre = mm(jnp.concatenate([senders, recvs_ref[...]], axis=1), wei_ref[...])
    act, slope = act_and_slope(pre)
    act = act.astype(bf16)
    act_ref[...] = act
    slope_ref[...] = slope.astype(bf16)
    message = mm(act, weo_ref[...]).astype(bf16).astype(f32)
    recv = live_row(recv_ref[...], first, count)
    acc[...] += put(recv, in_columns(recv), message, owned // LOW)

    @pl.when(step == pl.num_programs(0) - 1)
    def _():
        summed = tall(acc[...]).astype(bf16)
        summed_ref[...] = summed
        nodes = nodes_ref[...]
        pre = mm(jnp.concatenate([nodes, summed], axis=1), wni_ref[...])
        act, slope = act_and_slope(pre)
        act = act.astype(bf16)
        nact_ref[...] = act
        nslope_ref[...] = slope.astype(bf16)
        fine = (nodes.astype(f32) + mm(act, wno_ref[...])).astype(bf16)
        fine_ref[...] = fine
        rows = window_ref.shape[0]
        window = mm(one_hot_t(pool_ref[...], rows), fine)
        window_ref[...] = window
        wlow_ref[...] = window[: 2 * BAND].astype(bf16)
        whigh_ref[...] = window[rows - 2 * BAND :].astype(bf16)


def backward_kernel(
    send_ref,
    recv_ref,
    count_ref,
    senders_ref,
    recvs_ref,
    act_ref,
    slope_ref,
    window_ref,
    nlow_ref,
    nhigh_ref,
    dcl_ref,
    dch_ref,
    dcoarse_ref,
    dfine_ref,
    pool_ref,
    nodes_ref,
    summed_ref,
    nact_ref,
    nslope_ref,
    wei_ref,
    weo_ref,
    wni_ref,
    wno_ref,
    wci_ref,
    wco_ref,
    coarse_ref,
    dnode_ref,
    dedge_ref,
    rdown_ref,
    rup_ref,
    rown_ref,
    grads_ref,
    table,
    acc,
    gacc,
):
    step = pl.program_id(0)
    owned = nodes_ref.shape[0]

    @pl.when(step == 0)
    def _():
        acc[...] = jnp.zeros_like(acc)
        gacc[...] = jnp.zeros_like(gacc)
        window = window_ref[...]
        rows = window.shape[0]
        total = jnp.concatenate(
            [
                window[: 2 * BAND] + nlow_ref[...].astype(f32),
                window[2 * BAND : rows - 2 * BAND],
                window[rows - 2 * BAND :] + nhigh_ref[...].astype(f32),
            ],
            axis=0,
        )
        coarse_in = (0.125 * total).astype(bf16)
        d_coarse = jnp.concatenate([dcl_ref[...], dcoarse_ref[...], dch_ref[...]], axis=0)
        act, slope = act_and_slope(mm(coarse_in, wci_ref[...]))
        act = act.astype(bf16)
        coarse_out = (coarse_in.astype(f32) + mm(act, wco_ref[...])).astype(bf16)
        coarse_ref[...] = coarse_out[BAND : rows - BAND]
        d_pre = (mm_nt(d_coarse, wco_ref[...]) * slope).astype(bf16)
        d_in = (d_coarse.astype(f32) + mm_nt(d_pre, wci_ref[...])).astype(bf16)
        inner = slice(BAND, rows - BAND)
        g_ci = mm_tn(coarse_in[inner], d_pre[inner])
        g_co = mm_tn(act[inner], d_coarse[inner])
        reach = jnp.concatenate([d_in, jnp.zeros((2 * LAT - rows, LAT), bf16)], axis=0)
        parent = mm(one_hot(in_columns(pool_ref[...]), 2 * LAT), reach)
        d_total = dfine_ref[...].astype(f32) + 0.125 * parent
        d_out = d_total.astype(bf16)
        d_node = (mm_nt(d_out, wno_ref[...]) * nslope_ref[...].astype(f32)).astype(bf16)
        back = mm_nt(d_node, wni_ref[...])
        dnode_ref[...] = d_total + back[:, :LAT]
        table[...] = wide(back[:, LAT:].astype(bf16))
        g_ni = mm_tn(jnp.concatenate([nodes_ref[...], summed_ref[...]], axis=1), d_node)
        g_no = mm_tn(nact_ref[...], d_out)
        grads_ref[3 * LAT : 5 * LAT, :] = g_ni.astype(bf16)
        grads_ref[5 * LAT : 6 * LAT, :] = g_no.astype(bf16)
        grads_ref[6 * LAT : 7 * LAT, :] = g_ci.astype(bf16)
        grads_ref[7 * LAT :, :] = g_co.astype(bf16)

    first = step * STEP
    count = count_ref[0]
    recv = in_columns(live_row(recv_ref[...], first, count))
    d_message = take(recv, table[...]).astype(bf16)
    d_pre = (mm_nt(d_message, weo_ref[...]) * slope_ref[...].astype(f32)).astype(bf16)
    dedge_ref[...] = d_pre
    gacc[: 2 * LAT, :] += mm_tn(jnp.concatenate([senders_ref[...], recvs_ref[...]], axis=1), d_pre)
    gacc[2 * LAT :, :] += mm_tn(act_ref[...], d_message)
    send = live_row(send_ref[...], first, count) - owned
    acc[...] += put(send, in_columns(send), d_pre.astype(f32), 4)

    @pl.when(step == pl.num_programs(0) - 1)
    def _():
        grads_ref[: 3 * LAT, :] = gacc[...].astype(bf16)
        ghosts = mm_nt(tall(acc[...]).astype(bf16), wei_ref[:LAT, :]).astype(bf16)
        slots = ghosts.shape[0] // 8
        for place, (ref, i) in enumerate(
            (
                (rup_ref, 2),
                (rown_ref, 0),
                (rdown_ref, 2),
                (rup_ref, 1),
                (rdown_ref, 1),
                (rup_ref, 0),
                (rown_ref, 1),
                (rdown_ref, 0),
            )
        ):
            ref[i * slots : (i + 1) * slots, :] = ghosts[place * slots : (place + 1) * slots]


def local_kernel(count_ref, send_ref, recv_ref, dedge_ref, dnode_ref, wei_ref, out_ref, acc_s, acc_r):
    step = pl.program_id(0)

    @pl.when(step == 0)
    def _():
        acc_s[...] = jnp.zeros_like(acc_s)
        acc_r[...] = jnp.zeros_like(acc_r)

    first = step * STEP
    count = count_ref[0]
    groups = out_ref.shape[0] // LOW
    d_pre = dedge_ref[...].astype(f32)
    send = live_row(send_ref[...], first, count)
    recv = live_row(recv_ref[...], first, count)
    acc_s[...] += put(send, in_columns(send), d_pre, groups)
    acc_r[...] += put(recv, in_columns(recv), d_pre, groups)

    @pl.when(step == pl.num_programs(0) - 1)
    def _():
        out_ref[...] = (
            dnode_ref[...]
            + mm_nt(tall(acc_s[...]).astype(bf16), wei_ref[:LAT, :])
            + mm_nt(tall(acc_r[...]).astype(bf16), wei_ref[LAT:, :])
        )


def return_kernel(count_ref, rows_ref, down_ref, up_ref, mid_low_ref, mid_high_ref, part_ref, out_ref):
    slots = rows_ref.shape[2]
    groups = out_ref.shape[0] // LOW
    total = jnp.zeros((LOW, groups * LAT), f32)
    for k in range(8):
        row = live_row(rows_ref[0, k : k + 1, :], 0, count_ref[0, k])
        if k < 3:
            got = down_ref[k * slots : (k + 1) * slots, :]
        elif k == 3:
            got = mid_low_ref[slots : 2 * slots, :]
        elif k == 4:
            got = mid_high_ref[slots : 2 * slots, :]
        else:
            got = up_ref[(k - 5) * slots : (k - 4) * slots, :]
        total = total + put(row, in_columns(row), got.astype(f32), groups)
    out_ref[...] = part_ref[...] + tall(total)


def scale_kernel(scale, sums_ref, *out_refs):
    first = 0
    for ref in out_refs:
        rows = ref.shape[0]
        ref[...] = sums_ref[first : first + rows, :].astype(f32) * scale
        first += rows


def whole(shape):
    return pl.BlockSpec(shape, lambda *_: (0,) * len(shape))


def scalars():
    return pl.BlockSpec(memory_space=pltpu.SMEM)


def edge_row():
    return pl.BlockSpec((1, STEP), lambda i: (0, i))


def edge_block():
    return pl.BlockSpec((STEP, LAT), lambda i: (i, 0))


def shape(dims, dtype):
    return jax.ShapeDtypeStruct(dims, dtype)


def params(mib):
    return pltpu.CompilerParams(vmem_limit_bytes=mib * MIB)


def cost(flops, moved):
    return pl.CostEstimate(flops=flops, bytes_accessed=moved, transcendentals=0)


def reduced(grads):
    rows = grads.shape[0]
    far, near = GX, ("gy",)
    n_far, n_near = 32, 8
    part = rows // n_far
    got = lax.all_to_all(grads.reshape(n_far, part, LAT), far, 0, 0, tiled=True)
    own = got.astype(f32).sum(axis=0).astype(bf16)
    got = lax.all_to_all(jnp.broadcast_to(own[None], (n_near, part, LAT)), near, 0, 0, tiled=True)
    own = got.astype(f32).sum(axis=0).astype(bf16)
    got = lax.all_to_all(jnp.broadcast_to(own[None], (n_far, part, LAT)), far, 0, 0, tiled=True)
    return got.reshape(rows, LAT)


def body(
    nodes,
    ghost_rows,
    ghost_count,
    edge_send,
    edge_recv,
    edge_count,
    pool_map,
    w_edge_in,
    w_edge_out,
    w_node_in,
    w_node_out,
    w_coarse_in,
    w_coarse_out,
    d_fine,
    d_coarse,
):
    owned = nodes.shape[0]
    edges = edge_send.shape[1]
    slots = ghost_rows.shape[2]
    coarse = d_coarse.shape[0]
    window_rows = coarse + 2 * BAND
    steps = edges // STEP
    n_gx, n_gy = lax.axis_size(GX), lax.axis_size("gy")
    x_up = [(i, i + 1) for i in range(n_gx - 1)]
    x_down = [(j, i) for i, j in x_up]
    y_up = [(i, i + 1) for i in range(n_gy - 1)]
    y_down = [(j, i) for i, j in y_up]

    out_up, out_down, out_mid = pl.pallas_call(
        pick_kernel,
        out_shape=(
            shape((3 * slots, LAT), bf16),
            shape((3 * slots, LAT), bf16),
            shape((2 * slots, LAT), bf16),
        ),
        in_specs=[scalars(), whole(ghost_rows.shape), whole(nodes.shape)],
        out_specs=(whole((3 * slots, LAT)), whole((3 * slots, LAT)), whole((2 * slots, LAT))),
        grid=(1,),
        compiler_params=params(32),
        cost_estimate=cost(2 * 2048 * 512 * 256, MIB),
        name="pick",
    )(ghost_count, ghost_rows, nodes)

    up = lax.ppermute(out_up, GX, x_up)
    down = lax.ppermute(out_down, GX, x_down)

    sown, recvs = pl.pallas_call(
        own_kernel,
        grid=(steps,),
        out_shape=(shape((edges, LAT), bf16), shape((edges, LAT), bf16)),
        in_specs=[scalars(), edge_row(), edge_row(), whole(nodes.shape)],
        out_specs=(edge_block(), edge_block()),
        scratch_shapes=[pltpu.VMEM((LOW, owned // LOW * LAT), bf16)],
        compiler_params=params(32),
        cost_estimate=cost(2 * 2 * 4096 * 512 * 256, 3 * MIB),
        name="own_rows",
    )(edge_count, edge_send, edge_recv, nodes)

    yup = lax.ppermute(
        jnp.concatenate(
            [up[2 * slots :], out_mid[slots:], down[2 * slots :], d_coarse[coarse - BAND :]]
        ),
        "gy",
        y_up,
    )
    ydown = lax.ppermute(
        jnp.concatenate([up[:slots], out_mid[:slots], down[:slots], d_coarse[:BAND]]), "gy", y_down
    )

    edge16 = shape((edges, LAT), bf16)
    node16 = shape((owned, LAT), bf16)
    (
        senders,
        act,
        slope,
        fine_out,
        summed,
        nact,
        nslope,
        window,
        wlow,
        whigh,
    ) = pl.pallas_call(
        forward_kernel,
        grid=(steps,),
        out_shape=(
            edge16,
            edge16,
            edge16,
            node16,
            node16,
            node16,
            node16,
            shape((window_rows, LAT), f32),
            shape((2 * BAND, LAT), bf16),
            shape((2 * BAND, LAT), bf16),
        ),
        in_specs=[
            scalars(),
            edge_row(),
            edge_row(),
            edge_block(),
            edge_block(),
            whole(up.shape),
            whole(down.shape),
            whole(yup.shape),
            whole(ydown.shape),
            whole(nodes.shape),
            whole(pool_map.shape),
            whole(w_edge_in.shape),
            whole(w_edge_out.shape),
            whole(w_node_in.shape),
            whole(w_node_out.shape),
        ],
        out_specs=(
            edge_block(),
            edge_block(),
            edge_block(),
            whole((owned, LAT)),
            whole((owned, LAT)),
            whole((owned, LAT)),
            whole((owned, LAT)),
            whole((window_rows, LAT)),
            whole((2 * BAND, LAT)),
            whole((2 * BAND, LAT)),
        ),
        scratch_shapes=[
            pltpu.VMEM((LOW, 4 * LAT), bf16),
            pltpu.VMEM((LOW, owned // LOW * LAT), f32),
        ],
        compiler_params=params(32),
        cost_estimate=cost(2 * 4096 * 512 * 1024, 8 * MIB),
        name="forward",
    )(
        edge_count,
        edge_send,
        edge_recv,
        sown,
        recvs,
        up,
        down,
        yup,
        ydown,
        nodes,
        pool_map,
        w_edge_in,
        w_edge_out,
        w_node_in,
        w_node_out,
    )

    nlow = lax.ppermute(whigh, "gy", y_up)
    nhigh = lax.ppermute(wlow, "gy", y_down)
    d_low = yup[3 * slots :]
    d_high = ydown[3 * slots :]

    (coarse_out, d_node, d_edge, r_down, r_up, r_own, grads) = pl.pallas_call(
        backward_kernel,
        grid=(steps,),
        out_shape=(
            shape((coarse, LAT), bf16),
            shape((owned, LAT), f32),
            edge16,
            shape((3 * slots, LAT), bf16),
            shape((3 * slots, LAT), bf16),
            shape((2 * slots, LAT), bf16),
            shape((8 * LAT, LAT), bf16),
        ),
        in_specs=[
            edge_row(),
            edge_row(),
            scalars(),
            edge_block(),
            edge_block(),
            edge_block(),
            edge_block(),
            whole(window.shape),
            whole(nlow.shape),
            whole(nhigh.shape),
            whole(d_low.shape),
            whole(d_high.shape),
            whole(d_coarse.shape),
            whole(d_fine.shape),
            whole(pool_map.shape),
            whole(nodes.shape),
            whole(summed.shape),
            whole(nact.shape),
            whole(nslope.shape),
            whole(w_edge_in.shape),
            whole(w_edge_out.shape),
            whole(w_node_in.shape),
            whole(w_node_out.shape),
            whole(w_coarse_in.shape),
            whole(w_coarse_out.shape),
        ],
        out_specs=(
            whole((coarse, LAT)),
            whole((owned, LAT)),
            edge_block(),
            whole((3 * slots, LAT)),
            whole((3 * slots, LAT)),
            whole((2 * slots, LAT)),
            whole((8 * LAT, LAT)),
        ),
        scratch_shapes=[
            pltpu.VMEM((LOW, owned // LOW * LAT), bf16),
            pltpu.VMEM((LOW, 4 * LAT), f32),
            pltpu.VMEM((3 * LAT, LAT), f32),
        ],
        compiler_params=params(32),
        cost_estimate=cost(2 * 4096 * 512 * 1024, 8 * MIB),
        name="backward",
    )(
        edge_send,
        edge_recv,
        edge_count,
        senders,
        recvs,
        act,
        slope,
        window,
        nlow,
        nhigh,
        d_low,
        d_high,
        d_coarse,
        d_fine,
        pool_map,
        nodes,
        summed,
        nact,
        nslope,
        w_edge_in,
        w_edge_out,
        w_node_in,
        w_node_out,
        w_coarse_in,
        w_coarse_out,
    )

    high = lax.ppermute(r_down, "gy", y_down)
    low = lax.ppermute(r_up, "gy", y_up)

    d_own = pl.pallas_call(
        local_kernel,
        grid=(steps,),
        out_shape=shape((owned, LAT), f32),
        in_specs=[
            scalars(),
            edge_row(),
            edge_row(),
            edge_block(),
            whole((owned, LAT)),
            whole(w_edge_in.shape),
        ],
        out_specs=whole((owned, LAT)),
        scratch_shapes=[pltpu.VMEM((LOW, owned // LOW * LAT), f32)] * 2,
        compiler_params=params(32),
        cost_estimate=cost(2 * 2 * 4096 * 512 * 256, 3 * MIB),
        name="local",
    )(edge_count, edge_send, edge_recv, d_edge, d_node, w_edge_in)

    ret_up = lax.ppermute(
        jnp.concatenate([low[:slots], r_own[slots:], high[:slots]]), GX, x_down
    )
    ret_down = lax.ppermute(
        jnp.concatenate([low[2 * slots :], r_own[:slots], high[2 * slots :]]), GX, x_up
    )

    grad_nodes = pl.pallas_call(
        return_kernel,
        grid=(1,),
        out_shape=shape((owned, LAT), f32),
        in_specs=[
            scalars(),
            whole(ghost_rows.shape),
            whole(ret_down.shape),
            whole(ret_up.shape),
            whole(low.shape),
            whole(high.shape),
            whole(d_own.shape),
        ],
        out_specs=whole((owned, LAT)),
        compiler_params=params(32),
        cost_estimate=cost(2 * 2048 * 512 * 256, 2 * MIB),
        name="returned",
    )(ghost_count, ghost_rows, ret_down, ret_up, low, high, d_own)

    sums = reduced(grads)
    grad_scale = 1.0 / (owned * n_gx * n_gy) ** 0.5
    heights = (2 * LAT, LAT, 2 * LAT, LAT, LAT, LAT)
    scaled = pl.pallas_call(
        lambda *refs: scale_kernel(grad_scale, *refs),
        out_shape=tuple(shape((h, LAT), f32) for h in heights),
        name="scaled",
    )(sums)
    return (fine_out, coarse_out, grad_nodes, *scaled)


def solution(mesh):
    torus = Mesh(mesh.devices.reshape(4, 4, 2, mesh.shape["gy"]), GX_GY)
    in_specs = (
        P(GX_GY, None),
        P(GX_GY, None, None),
        P(GX_GY, None),
        P(GX_GY, None),
        P(GX_GY, None),
        P(GX_GY),
        P(GX_GY, None),
        P(),
        P(),
        P(),
        P(),
        P(),
        P(),
        P(GX_GY, None),
        P(GX_GY, None),
    )
    out_specs = (P(GX_GY, None), P(GX_GY, None), P(GX_GY, None), P(), P(), P(), P(), P(), P())
    return jax.shard_map(body, mesh=torus, in_specs=in_specs, out_specs=out_specs, check_vma=False)
```

```python
import jax
import jax.numpy as jnp
from jax import lax
from jax.experimental import pallas as pl
from jax.experimental.pallas import tpu as pltpu
from jax.sharding import Mesh
from jax.sharding import PartitionSpec as P

BAND = 32
LAT = 128
LOW = 512
BITS = 9
OWN_STEP = FWD_STEP = BWD_STEP = GHOST_STEP = LOCAL_STEP = 512
GX_GY = ("gx_0", "gx_1", "gx_2", "gy")
GX = ("gx_0", "gx_1", "gx_2")
ACROSS = (-1, -1, -1, 0, 0, 1, 1, 1)
ALONG = (-1, 0, 1, -1, 1, -1, 0, 1)
MIB = 1024 * 1024

f32 = jnp.float32
bf16 = jnp.bfloat16


def mm(left, right):
    return jnp.dot(left, right, preferred_element_type=f32)


def mm_nt(left, right):
    return lax.dot_general(left, right, (((1,), (1,)), ((), ())), preferred_element_type=f32)


def mm_tn(left, right):
    return lax.dot_general(left, right, (((0,), (0,)), ((), ())), preferred_element_type=f32)


def wide(table):
    groups = table.shape[0] // LOW
    return jnp.concatenate([table[i * LOW : (i + 1) * LOW] for i in range(groups)], axis=1)


def tall(table):
    groups = table.shape[1] // LAT
    return jnp.concatenate([table[:, i * LAT : (i + 1) * LAT] for i in range(groups)], axis=0)


def in_columns(row):
    parts = []
    for j in range(row.shape[1] // LAT):
        parts.append(jnp.broadcast_to(row[:, j * LAT : (j + 1) * LAT], (LAT, LAT)).T)
    return jnp.concatenate(parts, axis=0)


def one_hot(col, rows):
    lanes = lax.broadcasted_iota(jnp.int32, col.shape, 1)
    return jnp.concatenate(
        [(col == lanes + j * LAT).astype(f32).astype(bf16) for j in range(rows // LAT)], axis=1
    )


def one_hot_t(row, rows):
    ids = lax.broadcasted_iota(jnp.int32, (rows, row.shape[1]), 0)
    return (ids == row).astype(f32).astype(bf16)


def take(col, table):
    got = mm(one_hot(col & (LOW - 1), LOW), table)
    group = col >> BITS
    total = jnp.zeros((col.shape[0], LAT), f32)
    for i in range(table.shape[1] // LAT):
        total = jnp.where(group == i, got[:, i * LAT : (i + 1) * LAT], total)
    return total


def put(row, col, values, groups):
    group = col >> BITS
    spread = jnp.concatenate(
        [jnp.where(group == i, values, 0.0).astype(bf16) for i in range(groups)], axis=1
    )
    return mm(one_hot_t(row & (LOW - 1), LOW), spread)


def sigmoid(v):
    return 1.0 / (1.0 + jnp.exp(-v))


def act_and_slope(v):
    s = sigmoid(v)
    return v * s, s * (1.0 + v * (1.0 - s))


def live_row(row, first, count):
    ids = lax.broadcasted_iota(jnp.int32, row.shape, 1) + first
    return jnp.where(ids < count, row, -1)


def live_slots(place_ref, count_ref, k):
    a = place_ref[0] + ACROSS[k]
    b = place_ref[1] + ALONG[k]
    inside = (a >= 0) & (a < place_ref[2]) & (b >= 0) & (b < place_ref[3])
    return jnp.where(inside, count_ref[0, k], 0)


def pick_kernel(place_ref, count_ref, rows_hbm, nodes_hbm, up_ref, down_ref, mid_ref, rows, nodes, sems):
    copies = (
        pltpu.make_async_copy(nodes_hbm, nodes, sems.at[0]),
        pltpu.make_async_copy(rows_hbm, rows, sems.at[1]),
    )
    for copy in copies:
        copy.start()
    for copy in copies:
        copy.wait()
    table = wide(nodes[...])
    slots = rows.shape[2]
    for k in range(8):
        row = live_row(rows[0, k : k + 1, :], 0, live_slots(place_ref, count_ref, k))
        got = take(in_columns(row), table).astype(bf16)
        if k < 3:
            down_ref[k * slots : (k + 1) * slots, :] = got
        elif k < 5:
            mid_ref[(k - 3) * slots : (k - 2) * slots, :] = got
        else:
            up_ref[(k - 5) * slots : (k - 4) * slots, :] = got


def own_kernel(count_ref, index_ref, nodes_ref, out_ref):
    table = wide(nodes_ref[...])
    first = pl.program_id(0) * index_ref.shape[1]
    row = live_row(index_ref[...], first, count_ref[0])
    out_ref[...] = take(in_columns(row), table).astype(bf16)


def forward_kernel(
    count_ref,
    send_ref,
    recv_ref,
    sown_ref,
    recvs_ref,
    up_ref,
    down_ref,
    yup_ref,
    ydown_ref,
    nodes_ref,
    pool_ref,
    wei_ref,
    weo_ref,
    wni_ref,
    wno_ref,
    senders_ref,
    act_ref,
    slope_ref,
    fine_ref,
    summed_ref,
    nact_ref,
    nslope_ref,
    window_ref,
    wlow_ref,
    whigh_ref,
    table,
    acc,
):
    step = pl.program_id(0)
    slots = up_ref.shape[0] // 3

    @pl.when(step == 0)
    def _():
        def block(ref, i):
            return ref[i * slots : (i + 1) * slots, :]

        blocks = (
            block(ydown_ref, 2),
            block(down_ref, 1),
            block(yup_ref, 2),
            block(ydown_ref, 1),
            block(yup_ref, 1),
            block(ydown_ref, 0),
            block(up_ref, 1),
            block(yup_ref, 0),
        )
        for k in range(8):
            table[(k % 2) * slots : (k % 2 + 1) * slots, (k // 2) * LAT : (k // 2 + 1) * LAT] = blocks[k]
        acc[...] = jnp.zeros_like(acc)

    first = step * send_ref.shape[1]
    count = count_ref[0]
    owned = nodes_ref.shape[0]
    send = in_columns(live_row(send_ref[...], first, count)) - owned
    senders = (take(send, table[...]) + sown_ref[...].astype(f32)).astype(bf16)
    senders_ref[...] = senders
    pre = mm(jnp.concatenate([senders, recvs_ref[...]], axis=1), wei_ref[...])
    act, slope = act_and_slope(pre)
    act = act.astype(bf16)
    act_ref[...] = act
    slope_ref[...] = slope.astype(bf16)
    message = mm(act, weo_ref[...]).astype(bf16).astype(f32)
    recv = live_row(recv_ref[...], first, count)
    acc[...] += put(recv, in_columns(recv), message, owned // LOW)

    @pl.when(step == pl.num_programs(0) - 1)
    def _():
        summed = tall(acc[...]).astype(bf16)
        summed_ref[...] = summed
        nodes = nodes_ref[...]
        pre = mm(jnp.concatenate([nodes, summed], axis=1), wni_ref[...])
        act, slope = act_and_slope(pre)
        act = act.astype(bf16)
        nact_ref[...] = act
        nslope_ref[...] = slope.astype(bf16)
        fine = (nodes.astype(f32) + mm(act, wno_ref[...])).astype(bf16)
        fine_ref[...] = fine
        rows = window_ref.shape[0]
        window = mm(one_hot_t(pool_ref[...], rows), fine)
        window_ref[...] = window
        wlow_ref[...] = window[: 2 * BAND].astype(bf16)
        whigh_ref[...] = window[rows - 2 * BAND :].astype(bf16)


def backward_kernel(
    recv_ref,
    count_ref,
    senders_ref,
    recvs_ref,
    act_ref,
    slope_ref,
    window_ref,
    nlow_ref,
    nhigh_ref,
    dcl_ref,
    dch_ref,
    dcoarse_ref,
    dfine_ref,
    pool_ref,
    nodes_ref,
    summed_ref,
    nact_ref,
    nslope_ref,
    wei_ref,
    weo_ref,
    wni_ref,
    wno_ref,
    wci_ref,
    wco_ref,
    coarse_ref,
    dnode_ref,
    dedge_ref,
    grads_ref,
    table,
    gacc,
):
    step = pl.program_id(0)

    @pl.when(step == 0)
    def _():
        gacc[...] = jnp.zeros_like(gacc)
        window = window_ref[...]
        rows = window.shape[0]
        total = jnp.concatenate(
            [
                window[: 2 * BAND] + nlow_ref[...].astype(f32),
                window[2 * BAND : rows - 2 * BAND],
                window[rows - 2 * BAND :] + nhigh_ref[...].astype(f32),
            ],
            axis=0,
        )
        coarse_in = (0.125 * total).astype(bf16)
        d_coarse = jnp.concatenate([dcl_ref[...], dcoarse_ref[...], dch_ref[...]], axis=0)
        act, slope = act_and_slope(mm(coarse_in, wci_ref[...]))
        act = act.astype(bf16)
        coarse_out = (coarse_in.astype(f32) + mm(act, wco_ref[...])).astype(bf16)
        coarse_ref[...] = coarse_out[BAND : rows - BAND]
        d_pre = (mm_nt(d_coarse, wco_ref[...]) * slope).astype(bf16)
        d_in = (d_coarse.astype(f32) + mm_nt(d_pre, wci_ref[...])).astype(bf16)
        inner = slice(BAND, rows - BAND)
        g_ci = mm_tn(coarse_in[inner], d_pre[inner])
        g_co = mm_tn(act[inner], d_coarse[inner])
        reach = jnp.concatenate([d_in, jnp.zeros((2 * LAT - rows, LAT), bf16)], axis=0)
        parent = mm(one_hot(in_columns(pool_ref[...]), 2 * LAT), reach)
        d_total = dfine_ref[...].astype(f32) + 0.125 * parent
        d_out = d_total.astype(bf16)
        d_node = (mm_nt(d_out, wno_ref[...]) * nslope_ref[...].astype(f32)).astype(bf16)
        back = mm_nt(d_node, wni_ref[...])
        dnode_ref[...] = d_total + back[:, :LAT]
        table[...] = wide(back[:, LAT:].astype(bf16))
        g_ni = mm_tn(jnp.concatenate([nodes_ref[...], summed_ref[...]], axis=1), d_node)
        g_no = mm_tn(nact_ref[...], d_out)
        grads_ref[3 * LAT : 5 * LAT, :] = g_ni.astype(bf16)
        grads_ref[5 * LAT : 6 * LAT, :] = g_no.astype(bf16)
        grads_ref[6 * LAT : 7 * LAT, :] = g_ci.astype(bf16)
        grads_ref[7 * LAT :, :] = g_co.astype(bf16)

    first = step * recv_ref.shape[1]
    count = count_ref[0]
    recv = in_columns(live_row(recv_ref[...], first, count))
    d_message = take(recv, table[...]).astype(bf16)
    d_pre = (mm_nt(d_message, weo_ref[...]) * slope_ref[...].astype(f32)).astype(bf16)
    dedge_ref[...] = d_pre
    gacc[: 2 * LAT, :] += mm_tn(jnp.concatenate([senders_ref[...], recvs_ref[...]], axis=1), d_pre)
    gacc[2 * LAT :, :] += mm_tn(act_ref[...], d_message)

    @pl.when(step == pl.num_programs(0) - 1)
    def _():
        grads_ref[: 3 * LAT, :] = gacc[...].astype(bf16)


def ghost_kernel(
    count_ref, send_ref, dedge_ref, wei_ref, rdown_ref, rup_ref, rown_ref, acc, *, owned
):
    step = pl.program_id(0)

    @pl.when(step == 0)
    def _():
        acc[...] = jnp.zeros_like(acc)

    first = step * send_ref.shape[1]
    send = live_row(send_ref[...], first, count_ref[0]) - owned
    acc[...] += put(send, in_columns(send), dedge_ref[...].astype(f32), 4)

    @pl.when(step == pl.num_programs(0) - 1)
    def _():
        ghosts = mm_nt(tall(acc[...]).astype(bf16), wei_ref[:LAT, :]).astype(bf16)
        slots = ghosts.shape[0] // 8
        for place, (ref, i) in enumerate(
            (
                (rup_ref, 2),
                (rown_ref, 0),
                (rdown_ref, 2),
                (rup_ref, 1),
                (rdown_ref, 1),
                (rup_ref, 0),
                (rown_ref, 1),
                (rdown_ref, 0),
            )
        ):
            ref[i * slots : (i + 1) * slots, :] = ghosts[place * slots : (place + 1) * slots]


def local_kernel(count_ref, send_ref, recv_ref, dedge_ref, dnode_ref, wei_ref, out_ref, acc_s, acc_r):
    step = pl.program_id(0)

    @pl.when(step == 0)
    def _():
        acc_s[...] = jnp.zeros_like(acc_s)
        acc_r[...] = jnp.zeros_like(acc_r)

    first = step * send_ref.shape[1]
    count = count_ref[0]
    groups = out_ref.shape[0] // LOW
    d_pre = dedge_ref[...].astype(f32)
    send = live_row(send_ref[...], first, count)
    recv = live_row(recv_ref[...], first, count)
    acc_s[...] += put(send, in_columns(send), d_pre, groups)
    acc_r[...] += put(recv, in_columns(recv), d_pre, groups)

    @pl.when(step == pl.num_programs(0) - 1)
    def _():
        out_ref[...] = (
            dnode_ref[...]
            + mm_nt(tall(acc_s[...]).astype(bf16), wei_ref[:LAT, :])
            + mm_nt(tall(acc_r[...]).astype(bf16), wei_ref[LAT:, :])
        )


def final_kernel(
    scale,
    place_ref,
    count_ref,
    rows_ref,
    down_ref,
    up_ref,
    mid_low_ref,
    mid_high_ref,
    part_ref,
    sums_ref,
    out_ref,
    *grad_refs,
):
    slots = rows_ref.shape[2]
    groups = out_ref.shape[0] // LOW
    total = jnp.zeros((LOW, groups * LAT), f32)
    for k in range(8):
        row = live_row(rows_ref[0, k : k + 1, :], 0, live_slots(place_ref, count_ref, k))
        if k < 3:
            got = down_ref[k * slots : (k + 1) * slots, :]
        elif k == 3:
            got = mid_low_ref[slots : 2 * slots, :]
        elif k == 4:
            got = mid_high_ref[slots : 2 * slots, :]
        else:
            got = up_ref[(k - 5) * slots : (k - 4) * slots, :]
        total = total + put(row, in_columns(row), got.astype(f32), groups)
    out_ref[...] = part_ref[...] + tall(total)
    first = 0
    for ref in grad_refs:
        rows = ref.shape[0]
        ref[...] = sums_ref[first : first + rows, :].astype(f32) * scale
        first += rows


def whole(shape):
    return pl.BlockSpec(shape, lambda *_: (0,) * len(shape))


def scalars():
    return pl.BlockSpec(memory_space=pltpu.SMEM)


def edge_row(step):
    return pl.BlockSpec((1, step), lambda i: (0, i))


def edge_block(step):
    return pl.BlockSpec((step, LAT), lambda i: (i, 0))


def hbm():
    return pl.BlockSpec(memory_space=pltpu.HBM)


def shape(dims, dtype):
    return jax.ShapeDtypeStruct(dims, dtype)


def params(mib):
    return pltpu.CompilerParams(vmem_limit_bytes=mib * MIB)


def cost(flops, moved):
    return pl.CostEstimate(flops=flops, bytes_accessed=moved, transcendentals=0)


def reduced(grads):
    rows = grads.shape[0]
    far, near = GX, ("gy",)
    n_far, n_near = 32, 8
    part = rows // n_far
    got = lax.all_to_all(grads.reshape(n_far, part, LAT), far, 0, 0, tiled=True)
    own = got.astype(f32).sum(axis=0).astype(bf16)
    got = lax.all_to_all(jnp.broadcast_to(own[None], (n_near, part, LAT)), near, 0, 0, tiled=True)
    own = got.astype(f32).sum(axis=0).astype(bf16)
    got = lax.all_to_all(jnp.broadcast_to(own[None], (n_far, part, LAT)), far, 0, 0, tiled=True)
    return got.reshape(rows, LAT)


def call_pick(place, ghost_count, ghost_rows, nodes):
    slots = ghost_rows.shape[2]
    return pl.pallas_call(
        pick_kernel,
        out_shape=(
            shape((3 * slots, LAT), bf16),
            shape((3 * slots, LAT), bf16),
            shape((2 * slots, LAT), bf16),
        ),
        in_specs=[scalars(), scalars(), hbm(), hbm()],
        scratch_shapes=[
            pltpu.VMEM(ghost_rows.shape, jnp.int32),
            pltpu.VMEM(nodes.shape, bf16),
            pltpu.SemaphoreType.DMA((2,)),
        ],
        compiler_params=params(32),
        cost_estimate=cost(2 * 2048 * 512 * 256, MIB),
        name="pick",
    )(place, ghost_count, ghost_rows, nodes)


def call_own(edge_count, index, nodes):
    edges = index.shape[1]
    step = OWN_STEP
    return pl.pallas_call(
        own_kernel,
        grid=(edges // step,),
        out_shape=shape((edges, LAT), bf16),
        in_specs=[scalars(), edge_row(step), whole(nodes.shape)],
        out_specs=edge_block(step),
        compiler_params=params(32),
        cost_estimate=cost(2 * 4096 * 512 * 256, 2 * MIB),
        name="own_rows",
    )(edge_count, index, nodes)


def call_forward(edge_count, send, recv, sown, recvs, up, down, yup, ydown, nodes, pool, rows, *weights):
    edges, owned, step = send.shape[1], nodes.shape[0], FWD_STEP
    edge16 = shape((edges, LAT), bf16)
    node16 = shape((owned, LAT), bf16)
    band = shape((2 * BAND, LAT), bf16)
    outs = (edge16,) * 3 + (node16,) * 4 + (shape((rows, LAT), f32), band, band)
    plain = (up, down, yup, ydown, nodes, pool, *weights)
    return pl.pallas_call(
        forward_kernel,
        grid=(edges // step,),
        out_shape=outs,
        in_specs=[
            scalars(),
            edge_row(step),
            edge_row(step),
            edge_block(step),
            edge_block(step),
            *(whole(x.shape) for x in plain),
        ],
        out_specs=(edge_block(step),) * 3 + tuple(whole(x.shape) for x in outs[3:]),
        scratch_shapes=[
            pltpu.VMEM((LOW, 4 * LAT), bf16),
            pltpu.VMEM((LOW, owned // LOW * LAT), f32),
        ],
        compiler_params=params(40),
        cost_estimate=cost(2 * 4096 * 512 * 1024, 8 * MIB),
        name="forward",
    )(edge_count, send, recv, sown, recvs, *plain)


def call_backward(recv, edge_count, edge_arrays, plain):
    edges, step = recv.shape[1], BWD_STEP
    owned, coarse = plain[8].shape[0], plain[5].shape[0]
    return pl.pallas_call(
        backward_kernel,
        grid=(edges // step,),
        out_shape=(
            shape((coarse, LAT), bf16),
            shape((owned, LAT), f32),
            shape((edges, LAT), bf16),
            shape((8 * LAT, LAT), bf16),
        ),
        in_specs=[
            edge_row(step),
            scalars(),
            *(edge_block(step) for _ in edge_arrays),
            *(whole(x.shape) for x in plain),
        ],
        out_specs=(
            whole((coarse, LAT)),
            whole((owned, LAT)),
            edge_block(step),
            whole((8 * LAT, LAT)),
        ),
        scratch_shapes=[
            pltpu.VMEM((LOW, owned // LOW * LAT), bf16),
            pltpu.VMEM((3 * LAT, LAT), f32),
        ],
        compiler_params=params(40),
        cost_estimate=cost(2 * 4096 * 512 * 512, 8 * MIB),
        name="backward",
    )(recv, edge_count, *edge_arrays, *plain)


def call_ghost(edge_count, send, d_edge, w_edge_in, owned, slots):
    edges, step = send.shape[1], GHOST_STEP
    outs = (
        shape((3 * slots, LAT), bf16),
        shape((3 * slots, LAT), bf16),
        shape((2 * slots, LAT), bf16),
    )
    return pl.pallas_call(
        lambda *refs: ghost_kernel(*refs, owned=owned),
        grid=(edges // step,),
        out_shape=outs,
        in_specs=[scalars(), edge_row(step), edge_block(step), whole(w_edge_in.shape)],
        out_specs=tuple(whole(x.shape) for x in outs),
        scratch_shapes=[pltpu.VMEM((LOW, 4 * LAT), f32)],
        compiler_params=params(32),
        cost_estimate=cost(2 * 4096 * 512 * 512, 3 * MIB),
        name="ghost_grads",
    )(edge_count, send, d_edge, w_edge_in)


def call_local(edge_count, send, recv, d_edge, d_node, w_edge_in):
    edges, step, owned = send.shape[1], LOCAL_STEP, d_node.shape[0]
    return pl.pallas_call(
        local_kernel,
        grid=(edges // step,),
        out_shape=shape((owned, LAT), f32),
        in_specs=[
            scalars(),
            edge_row(step),
            edge_row(step),
            edge_block(step),
            whole((owned, LAT)),
            whole(w_edge_in.shape),
        ],
        out_specs=whole((owned, LAT)),
        scratch_shapes=[pltpu.VMEM((LOW, owned // LOW * LAT), f32)] * 2,
        compiler_params=params(32),
        cost_estimate=cost(2 * 2 * 4096 * 512 * 256, 3 * MIB),
        name="local",
    )(edge_count, send, recv, d_edge, d_node, w_edge_in)


def call_final(scale, place, ghost_count, ghost_rows, *arrays):
    owned = arrays[4].shape[0]
    heights = (2 * LAT, LAT, 2 * LAT, LAT, LAT, LAT)
    return pl.pallas_call(
        lambda *refs: final_kernel(scale, *refs),
        out_shape=(shape((owned, LAT), f32), *(shape((h, LAT), f32) for h in heights)),
        in_specs=[
            scalars(),
            scalars(),
            whole(ghost_rows.shape),
            *(whole(x.shape) for x in arrays),
        ],
        compiler_params=params(32),
        cost_estimate=cost(2 * 2048 * 512 * 256, 2 * MIB),
        name="final",
    )(place, ghost_count, ghost_rows, *arrays)


def ring(n, shift):
    return [(i, (i + shift) % n) for i in range(n)]


def body(
    nodes,
    ghost_rows,
    ghost_count,
    edge_send,
    edge_recv,
    edge_count,
    pool_map,
    w_edge_in,
    w_edge_out,
    w_node_in,
    w_node_out,
    w_coarse_in,
    w_coarse_out,
    d_fine,
    d_coarse,
):
    owned = nodes.shape[0]
    slots = ghost_rows.shape[2]
    coarse = d_coarse.shape[0]
    n_gx, n_gy = lax.axis_size(GX), lax.axis_size("gy")
    place = jnp.stack([lax.axis_index(GX), lax.axis_index("gy"), n_gx, n_gy]).astype(jnp.int32)

    out_up, out_down, out_mid = call_pick(place, ghost_count, ghost_rows, nodes)
    up = lax.ppermute(out_up, GX, ring(n_gx, 1))
    down = lax.ppermute(out_down, GX, ring(n_gx, -1))
    recvs = call_own(edge_count, edge_recv, nodes)
    up, down, recvs = lax.optimization_barrier((up, down, recvs))

    yup = lax.ppermute(
        jnp.concatenate(
            [up[2 * slots :], out_mid[slots:], down[2 * slots :], d_coarse[coarse - BAND :]]
        ),
        "gy",
        ring(n_gy, 1),
    )
    ydown = lax.ppermute(
        jnp.concatenate([up[:slots], out_mid[:slots], down[:slots], d_coarse[:BAND]]),
        "gy",
        ring(n_gy, -1),
    )
    sown = call_own(edge_count, edge_send, nodes)

    (senders, act, slope, fine_out, summed, nact, nslope, window, wlow, whigh) = call_forward(
        edge_count,
        edge_send,
        edge_recv,
        sown,
        recvs,
        up,
        down,
        yup,
        ydown,
        nodes,
        pool_map,
        coarse + 2 * BAND,
        w_edge_in,
        w_edge_out,
        w_node_in,
        w_node_out,
    )

    nlow = lax.ppermute(whigh, "gy", ring(n_gy, 1))
    nhigh = lax.ppermute(wlow, "gy", ring(n_gy, -1))

    coarse_out, d_node, d_edge, grads = call_backward(
        edge_recv,
        edge_count,
        (senders, recvs, act, slope),
        (
            window,
            nlow,
            nhigh,
            yup[3 * slots :],
            ydown[3 * slots :],
            d_coarse,
            d_fine,
            pool_map,
            nodes,
            summed,
            nact,
            nslope,
            w_edge_in,
            w_edge_out,
            w_node_in,
            w_node_out,
            w_coarse_in,
            w_coarse_out,
        ),
    )
    r_down, r_up, r_own = call_ghost(edge_count, edge_send, d_edge, w_edge_in, owned, slots)
    high = lax.ppermute(r_down, "gy", ring(n_gy, -1))
    low = lax.ppermute(r_up, "gy", ring(n_gy, 1))
    d_own = call_local(edge_count, edge_send, edge_recv, d_edge, d_node, w_edge_in)
    high, low, d_own = lax.optimization_barrier((high, low, d_own))

    ret_up = lax.ppermute(
        jnp.concatenate([low[:slots], r_own[slots:], high[:slots]]), GX, ring(n_gx, -1)
    )
    ret_down = lax.ppermute(
        jnp.concatenate([low[2 * slots :], r_own[:slots], high[2 * slots :]]), GX, ring(n_gx, 1)
    )

    sums = reduced(grads)
    grad_scale = 1.0 / (owned * n_gx * n_gy) ** 0.5
    grad_nodes, *scaled = call_final(
        grad_scale, place, ghost_count, ghost_rows, ret_down, ret_up, low, high, d_own, sums
    )
    return (fine_out, coarse_out, grad_nodes, *scaled)


def solution(mesh):
    torus = Mesh(mesh.devices.reshape(4, 4, 2, mesh.shape["gy"]), GX_GY)
    in_specs = (
        P(GX_GY, None),
        P(GX_GY, None, None),
        P(GX_GY, None),
        P(GX_GY, None),
        P(GX_GY, None),
        P(GX_GY),
        P(GX_GY, None),
        P(),
        P(),
        P(),
        P(),
        P(),
        P(),
        P(GX_GY, None),
        P(GX_GY, None),
    )
    out_specs = (P(GX_GY, None), P(GX_GY, None), P(GX_GY, None), P(), P(), P(), P(), P(), P())
    return jax.shard_map(body, mesh=torus, in_specs=in_specs, out_specs=out_specs, check_vma=False)
```

```python
import jax
import jax.numpy as jnp
from jax import lax
from jax.experimental import pallas as pl
from jax.experimental.pallas import tpu as pltpu
from jax.sharding import Mesh
from jax.sharding import PartitionSpec as P

BAND = 32
LAT = 128
LOW = 512
BITS = 9
OWN_STEP = FWD_STEP = BWD_STEP = GHOST_STEP = LOCAL_STEP = 4096
GX_GY = ("gx_0", "gx_1", "gx_2", "gy")
GX = ("gx_0", "gx_1", "gx_2")
ACROSS = (-1, -1, -1, 0, 0, 1, 1, 1)
ALONG = (-1, 0, 1, -1, 1, -1, 0, 1)
MIB = 1024 * 1024

f32 = jnp.float32
bf16 = jnp.bfloat16


def mm(left, right):
    return jnp.dot(left, right, preferred_element_type=f32)


def mm_nt(left, right):
    return lax.dot_general(left, right, (((1,), (1,)), ((), ())), preferred_element_type=f32)


def mm_tn(left, right):
    return lax.dot_general(left, right, (((0,), (0,)), ((), ())), preferred_element_type=f32)


def wide(table):
    groups = table.shape[0] // LOW
    return jnp.concatenate([table[i * LOW : (i + 1) * LOW] for i in range(groups)], axis=1)


def tall(table):
    groups = table.shape[1] // LAT
    return jnp.concatenate([table[:, i * LAT : (i + 1) * LAT] for i in range(groups)], axis=0)


def in_columns(row):
    parts = []
    for j in range(row.shape[1] // LAT):
        parts.append(jnp.broadcast_to(row[:, j * LAT : (j + 1) * LAT], (LAT, LAT)).T)
    return jnp.concatenate(parts, axis=0).astype(jnp.int16)


def one_hot(col, rows):
    lanes = lax.broadcasted_iota(jnp.int16, col.shape, 1)
    one, zero = jnp.ones((), bf16), jnp.zeros((), bf16)
    return jnp.concatenate(
        [jnp.where(col == lanes + j * LAT, one, zero) for j in range(rows // LAT)], axis=1
    )


def one_hot_t(row, rows):
    ids = lax.broadcasted_iota(jnp.int16, (rows, row.shape[1]), 0)
    col = jnp.broadcast_to(row, (16, row.shape[1])).astype(jnp.int16)
    col = jnp.concatenate([col] * (rows // 16), axis=0)
    return jnp.where(ids == col, jnp.ones((), bf16), jnp.zeros((), bf16))


def take(col, table):
    got = mm(one_hot(col & (LOW - 1), LOW), table).astype(bf16)
    group = col >> BITS
    total = jnp.zeros((col.shape[0], LAT), bf16)
    for i in range(table.shape[1] // LAT):
        total = jnp.where(group == i, got[:, i * LAT : (i + 1) * LAT], total)
    return total


def put(row, col, values, groups):
    group = col >> BITS
    zero = jnp.zeros((), bf16)
    spread = jnp.concatenate([jnp.where(group == i, values, zero) for i in range(groups)], axis=1)
    return mm(one_hot_t(row & (LOW - 1), LOW), spread)


def sigmoid(v):
    return 0.5 + 0.5 * jnp.tanh(0.5 * v)


def act_and_slope(v):
    s = sigmoid(v)
    return v * s, s * (1.0 + v * (1.0 - s))


def live_row(row, first, count):
    ids = lax.broadcasted_iota(jnp.int32, row.shape, 1) + first
    return jnp.where(ids < count, row, -1)


def live_slots(place_ref, count_ref, k):
    a = place_ref[0] + ACROSS[k]
    b = place_ref[1] + ALONG[k]
    inside = (a >= 0) & (a < place_ref[2]) & (b >= 0) & (b < place_ref[3])
    return jnp.where(inside, count_ref[0, k], 0)


def pick_kernel(place_ref, count_ref, rows_hbm, nodes_hbm, up_ref, down_ref, mid_ref, cols_ref, rows, nodes, sems):
    copies = (
        pltpu.make_async_copy(nodes_hbm, nodes, sems.at[0]),
        pltpu.make_async_copy(rows_hbm, rows, sems.at[1]),
    )
    for copy in copies:
        copy.start()
    for copy in copies:
        copy.wait()
    table = wide(nodes[...])
    slots = rows.shape[2]
    for k in range(8):
        row = live_row(rows[0, k : k + 1, :], 0, live_slots(place_ref, count_ref, k))
        col = in_columns(row)
        cols_ref[k * slots : (k + 1) * slots, :] = col
        got = take(col, table)
        if k < 3:
            down_ref[k * slots : (k + 1) * slots, :] = got
        elif k < 5:
            mid_ref[(k - 3) * slots : (k - 2) * slots, :] = got
        else:
            up_ref[(k - 5) * slots : (k - 4) * slots, :] = got


def own_kernel(count_ref, index_ref, nodes_ref, out_ref, cols_ref):
    table = wide(nodes_ref[...])
    first = pl.program_id(0) * index_ref.shape[1]
    col = in_columns(live_row(index_ref[...], first, count_ref[0]))
    cols_ref[...] = col
    out_ref[...] = take(col, table)


def forward_kernel(
    count_ref,
    recv_ref,
    scol_ref,
    rcol_ref,
    sown_ref,
    recvs_ref,
    up_ref,
    down_ref,
    yup_ref,
    ydown_ref,
    nodes_ref,
    pool_ref,
    wei_ref,
    weo_ref,
    wni_ref,
    wno_ref,
    senders_ref,
    act_ref,
    slope_ref,
    fine_ref,
    summed_ref,
    nact_ref,
    nslope_ref,
    window_ref,
    wlow_ref,
    whigh_ref,
    table,
    acc,
):
    step = pl.program_id(0)
    slots = up_ref.shape[0] // 3

    @pl.when(step == 0)
    def _():
        def block(ref, i):
            return ref[i * slots : (i + 1) * slots, :]

        blocks = (
            block(ydown_ref, 2),
            block(down_ref, 1),
            block(yup_ref, 2),
            block(ydown_ref, 1),
            block(yup_ref, 1),
            block(ydown_ref, 0),
            block(up_ref, 1),
            block(yup_ref, 0),
        )
        for k in range(8):
            table[(k % 2) * slots : (k % 2 + 1) * slots, (k // 2) * LAT : (k // 2 + 1) * LAT] = blocks[k]
        acc[...] = jnp.zeros_like(acc)

    owned = nodes_ref.shape[0]
    senders = take(scol_ref[...] - owned, table[...]) + sown_ref[...]
    senders_ref[...] = senders
    pre = mm(jnp.concatenate([senders, recvs_ref[...]], axis=1), wei_ref[...])
    act, slope = act_and_slope(pre)
    act = act.astype(bf16)
    act_ref[...] = act
    slope_ref[...] = slope.astype(bf16)
    message = mm(act, weo_ref[...]).astype(bf16)
    recv = live_row(recv_ref[...], step * recv_ref.shape[1], count_ref[0])
    acc[...] += put(recv, rcol_ref[...], message, owned // LOW)

    @pl.when(step == pl.num_programs(0) - 1)
    def _():
        summed = tall(acc[...]).astype(bf16)
        summed_ref[...] = summed
        nodes = nodes_ref[...]
        pre = mm(jnp.concatenate([nodes, summed], axis=1), wni_ref[...])
        act, slope = act_and_slope(pre)
        act = act.astype(bf16)
        nact_ref[...] = act
        nslope_ref[...] = slope.astype(bf16)
        fine = (nodes.astype(f32) + mm(act, wno_ref[...])).astype(bf16)
        fine_ref[...] = fine
        rows = window_ref.shape[0]
        window = mm(one_hot_t(pool_ref[...], rows), fine)
        window_ref[...] = window
        wlow_ref[...] = window[: 2 * BAND].astype(bf16)
        whigh_ref[...] = window[rows - 2 * BAND :].astype(bf16)


def backward_kernel(
    rcol_ref,
    senders_ref,
    recvs_ref,
    act_ref,
    slope_ref,
    window_ref,
    nlow_ref,
    nhigh_ref,
    dcl_ref,
    dch_ref,
    dcoarse_ref,
    dfine_ref,
    pool_ref,
    nodes_ref,
    summed_ref,
    nact_ref,
    nslope_ref,
    wei_ref,
    weo_ref,
    wni_ref,
    wno_ref,
    wci_ref,
    wco_ref,
    coarse_ref,
    dnode_ref,
    dedge_ref,
    grads_ref,
    table,
    gacc,
):
    step = pl.program_id(0)

    @pl.when(step == 0)
    def _():
        gacc[...] = jnp.zeros_like(gacc)
        window = window_ref[...]
        rows = window.shape[0]
        total = jnp.concatenate(
            [
                window[: 2 * BAND] + nlow_ref[...].astype(f32),
                window[2 * BAND : rows - 2 * BAND],
                window[rows - 2 * BAND :] + nhigh_ref[...].astype(f32),
            ],
            axis=0,
        )
        coarse_in = (0.125 * total).astype(bf16)
        d_coarse = jnp.concatenate([dcl_ref[...], dcoarse_ref[...], dch_ref[...]], axis=0)
        act, slope = act_and_slope(mm(coarse_in, wci_ref[...]))
        act = act.astype(bf16)
        coarse_out = (coarse_in.astype(f32) + mm(act, wco_ref[...])).astype(bf16)
        coarse_ref[...] = coarse_out[BAND : rows - BAND]
        d_pre = (mm_nt(d_coarse, wco_ref[...]) * slope).astype(bf16)
        d_in = (d_coarse.astype(f32) + mm_nt(d_pre, wci_ref[...])).astype(bf16)
        inner = slice(BAND, rows - BAND)
        g_ci = mm_tn(coarse_in[inner], d_pre[inner])
        g_co = mm_tn(act[inner], d_coarse[inner])
        reach = jnp.concatenate([d_in, jnp.zeros((2 * LAT - rows, LAT), bf16)], axis=0)
        parent = mm(one_hot(in_columns(pool_ref[...]), 2 * LAT), reach)
        d_total = dfine_ref[...].astype(f32) + 0.125 * parent
        d_out = d_total.astype(bf16)
        d_node = (mm_nt(d_out, wno_ref[...]) * nslope_ref[...].astype(f32)).astype(bf16)
        back = mm_nt(d_node, wni_ref[...])
        dnode_ref[...] = d_total + back[:, :LAT]
        table[...] = wide(back[:, LAT:].astype(bf16))
        g_ni = mm_tn(jnp.concatenate([nodes_ref[...], summed_ref[...]], axis=1), d_node)
        g_no = mm_tn(nact_ref[...], d_out)
        grads_ref[3 * LAT : 5 * LAT, :] = g_ni.astype(bf16)
        grads_ref[5 * LAT : 6 * LAT, :] = g_no.astype(bf16)
        grads_ref[6 * LAT : 7 * LAT, :] = g_ci.astype(bf16)
        grads_ref[7 * LAT :, :] = g_co.astype(bf16)

    d_message = take(rcol_ref[...], table[...])
    d_pre = (mm_nt(d_message, weo_ref[...]) * slope_ref[...].astype(f32)).astype(bf16)
    dedge_ref[...] = d_pre
    gacc[: 2 * LAT, :] += mm_tn(jnp.concatenate([senders_ref[...], recvs_ref[...]], axis=1), d_pre)
    gacc[2 * LAT :, :] += mm_tn(act_ref[...], d_message)

    @pl.when(step == pl.num_programs(0) - 1)
    def _():
        grads_ref[: 3 * LAT, :] = gacc[...].astype(bf16)


def ghost_kernel(
    count_ref, send_ref, scol_ref, dedge_ref, wei_ref, rdown_ref, rup_ref, rown_ref, acc, *, owned
):
    step = pl.program_id(0)

    @pl.when(step == 0)
    def _():
        acc[...] = jnp.zeros_like(acc)

    first = step * send_ref.shape[1]
    send = live_row(send_ref[...], first, count_ref[0]) - owned
    acc[...] += put(send, scol_ref[...] - owned, dedge_ref[...], 4)

    @pl.when(step == pl.num_programs(0) - 1)
    def _():
        ghosts = mm_nt(tall(acc[...]).astype(bf16), wei_ref[:LAT, :]).astype(bf16)
        slots = ghosts.shape[0] // 8
        for place, (ref, i) in enumerate(
            (
                (rup_ref, 2),
                (rown_ref, 0),
                (rdown_ref, 2),
                (rup_ref, 1),
                (rdown_ref, 1),
                (rup_ref, 0),
                (rown_ref, 1),
                (rdown_ref, 0),
            )
        ):
            ref[i * slots : (i + 1) * slots, :] = ghosts[place * slots : (place + 1) * slots]


def local_kernel(count_ref, send_ref, recv_ref, scol_ref, rcol_ref, dedge_ref, dnode_ref, wei_ref, out_ref, acc_s, acc_r):
    step = pl.program_id(0)

    @pl.when(step == 0)
    def _():
        acc_s[...] = jnp.zeros_like(acc_s)
        acc_r[...] = jnp.zeros_like(acc_r)

    first = step * send_ref.shape[1]
    count = count_ref[0]
    groups = out_ref.shape[0] // LOW
    d_pre = dedge_ref[...]
    send = live_row(send_ref[...], first, count)
    recv = live_row(recv_ref[...], first, count)
    acc_s[...] += put(send, scol_ref[...], d_pre, groups)
    acc_r[...] += put(recv, rcol_ref[...], d_pre, groups)

    @pl.when(step == pl.num_programs(0) - 1)
    def _():
        out_ref[...] = (
            dnode_ref[...]
            + mm_nt(tall(acc_s[...]).astype(bf16), wei_ref[:LAT, :])
            + mm_nt(tall(acc_r[...]).astype(bf16), wei_ref[LAT:, :])
        )


def final_kernel(
    scale,
    place_ref,
    count_ref,
    rows_ref,
    cols_ref,
    down_ref,
    up_ref,
    mid_low_ref,
    mid_high_ref,
    part_ref,
    sums_ref,
    out_ref,
    *grad_refs,
):
    slots = rows_ref.shape[2]
    groups = out_ref.shape[0] // LOW
    total = jnp.zeros((LOW, groups * LAT), f32)
    for k in range(8):
        row = live_row(rows_ref[0, k : k + 1, :], 0, live_slots(place_ref, count_ref, k))
        col = cols_ref[k * slots : (k + 1) * slots, :]
        if k < 3:
            got = down_ref[k * slots : (k + 1) * slots, :]
        elif k == 3:
            got = mid_low_ref[slots : 2 * slots, :]
        elif k == 4:
            got = mid_high_ref[slots : 2 * slots, :]
        else:
            got = up_ref[(k - 5) * slots : (k - 4) * slots, :]
        total = total + put(row, col, got, groups)
    out_ref[...] = part_ref[...] + tall(total)
    first = 0
    for ref in grad_refs:
        rows = ref.shape[0]
        ref[...] = sums_ref[first : first + rows, :].astype(f32) * scale
        first += rows


def whole(shape):
    return pl.BlockSpec(shape, lambda *_: (0,) * len(shape))


def scalars():
    return pl.BlockSpec(memory_space=pltpu.SMEM)


def edge_row(step):
    return pl.BlockSpec((1, step), lambda i: (0, i))


def edge_block(step):
    return pl.BlockSpec((step, LAT), lambda i: (i, 0))


def hbm():
    return pl.BlockSpec(memory_space=pltpu.HBM)


def shape(dims, dtype):
    return jax.ShapeDtypeStruct(dims, dtype)


def params(mib):
    return pltpu.CompilerParams(vmem_limit_bytes=mib * MIB)


def cost(flops, moved):
    return pl.CostEstimate(flops=flops, bytes_accessed=moved, transcendentals=0)


def reduced(grads):
    rows = grads.shape[0]
    far, near = GX, ("gy",)
    n_far, n_near = 32, 8
    part = rows // n_far
    got = lax.all_to_all(grads.reshape(n_far, part, LAT), far, 0, 0, tiled=True)
    own = got.astype(f32).sum(axis=0).astype(bf16)
    got = lax.all_to_all(jnp.broadcast_to(own[None], (n_near, part, LAT)), near, 0, 0, tiled=True)
    own = got.astype(f32).sum(axis=0).astype(bf16)
    got = lax.all_to_all(jnp.broadcast_to(own[None], (n_far, part, LAT)), far, 0, 0, tiled=True)
    return got.reshape(rows, LAT)


def call_pick(place, ghost_count, ghost_rows, nodes):
    slots = ghost_rows.shape[2]
    return pl.pallas_call(
        pick_kernel,
        out_shape=(
            shape((3 * slots, LAT), bf16),
            shape((3 * slots, LAT), bf16),
            shape((2 * slots, LAT), bf16),
            shape((8 * slots, LAT), jnp.int16),
        ),
        in_specs=[scalars(), scalars(), hbm(), hbm()],
        scratch_shapes=[
            pltpu.VMEM(ghost_rows.shape, jnp.int32),
            pltpu.VMEM(nodes.shape, bf16),
            pltpu.SemaphoreType.DMA((2,)),
        ],
        compiler_params=params(32),
        cost_estimate=cost(2 * 2048 * 512 * 256, MIB),
        name="pick",
    )(place, ghost_count, ghost_rows, nodes)


def call_own(edge_count, index, nodes):
    edges = index.shape[1]
    step = OWN_STEP
    return pl.pallas_call(
        own_kernel,
        grid=(edges // step,),
        out_shape=(shape((edges, LAT), bf16), shape((edges, LAT), jnp.int16)),
        in_specs=[scalars(), edge_row(step), whole(nodes.shape)],
        out_specs=(edge_block(step), edge_block(step)),
        compiler_params=params(32),
        cost_estimate=cost(2 * 4096 * 512 * 256, 2 * MIB),
        name="own_rows",
    )(edge_count, index, nodes)


def call_forward(edge_count, recv, scol, rcol, sown, recvs, up, down, yup, ydown, nodes, pool, rows, *weights):
    edges, owned, step = recv.shape[1], nodes.shape[0], FWD_STEP
    edge16 = shape((edges, LAT), bf16)
    node16 = shape((owned, LAT), bf16)
    band = shape((2 * BAND, LAT), bf16)
    outs = (edge16,) * 3 + (node16,) * 4 + (shape((rows, LAT), f32), band, band)
    plain = (up, down, yup, ydown, nodes, pool, *weights)
    return pl.pallas_call(
        forward_kernel,
        grid=(edges // step,),
        out_shape=outs,
        in_specs=[
            scalars(),
            edge_row(step),
            edge_block(step),
            edge_block(step),
            edge_block(step),
            edge_block(step),
            *(whole(x.shape) for x in plain),
        ],
        out_specs=(edge_block(step),) * 3 + tuple(whole(x.shape) for x in outs[3:]),
        scratch_shapes=[
            pltpu.VMEM((LOW, 4 * LAT), bf16),
            pltpu.VMEM((LOW, owned // LOW * LAT), f32),
        ],
        compiler_params=params(40),
        cost_estimate=cost(2 * 4096 * 512 * 1024, 8 * MIB),
        name="forward",
    )(edge_count, recv, scol, rcol, sown, recvs, *plain)


def call_backward(edge_arrays, plain):
    edges, step = edge_arrays[0].shape[0], BWD_STEP
    owned, coarse = plain[8].shape[0], plain[5].shape[0]
    return pl.pallas_call(
        backward_kernel,
        grid=(edges // step,),
        out_shape=(
            shape((coarse, LAT), bf16),
            shape((owned, LAT), f32),
            shape((edges, LAT), bf16),
            shape((8 * LAT, LAT), bf16),
        ),
        in_specs=[
            *(edge_block(step) for _ in edge_arrays),
            *(whole(x.shape) for x in plain),
        ],
        out_specs=(
            whole((coarse, LAT)),
            whole((owned, LAT)),
            edge_block(step),
            whole((8 * LAT, LAT)),
        ),
        scratch_shapes=[
            pltpu.VMEM((LOW, owned // LOW * LAT), bf16),
            pltpu.VMEM((3 * LAT, LAT), f32),
        ],
        compiler_params=params(40),
        cost_estimate=cost(2 * 4096 * 512 * 512, 8 * MIB),
        name="backward",
    )(*edge_arrays, *plain)


def call_ghost(edge_count, send, scol, d_edge, w_edge_in, owned, slots):
    edges, step = send.shape[1], GHOST_STEP
    outs = (
        shape((3 * slots, LAT), bf16),
        shape((3 * slots, LAT), bf16),
        shape((2 * slots, LAT), bf16),
    )
    return pl.pallas_call(
        lambda *refs: ghost_kernel(*refs, owned=owned),
        grid=(edges // step,),
        out_shape=outs,
        in_specs=[
            scalars(),
            edge_row(step),
            edge_block(step),
            edge_block(step),
            whole(w_edge_in.shape),
        ],
        out_specs=tuple(whole(x.shape) for x in outs),
        scratch_shapes=[pltpu.VMEM((LOW, 4 * LAT), f32)],
        compiler_params=params(32),
        cost_estimate=cost(2 * 4096 * 512 * 512, 3 * MIB),
        name="ghost_grads",
    )(edge_count, send, scol, d_edge, w_edge_in)


def call_local(edge_count, send, recv, scol, rcol, d_edge, d_node, w_edge_in):
    edges, step, owned = send.shape[1], LOCAL_STEP, d_node.shape[0]
    return pl.pallas_call(
        local_kernel,
        grid=(edges // step,),
        out_shape=shape((owned, LAT), f32),
        in_specs=[
            scalars(),
            edge_row(step),
            edge_row(step),
            edge_block(step),
            edge_block(step),
            edge_block(step),
            whole((owned, LAT)),
            whole(w_edge_in.shape),
        ],
        out_specs=whole((owned, LAT)),
        scratch_shapes=[pltpu.VMEM((LOW, owned // LOW * LAT), f32)] * 2,
        compiler_params=params(32),
        cost_estimate=cost(2 * 2 * 4096 * 512 * 256, 3 * MIB),
        name="local",
    )(edge_count, send, recv, scol, rcol, d_edge, d_node, w_edge_in)


def call_final(scale, place, ghost_count, ghost_rows, *arrays):
    owned = arrays[5].shape[0]
    heights = (2 * LAT, LAT, 2 * LAT, LAT, LAT, LAT)
    return pl.pallas_call(
        lambda *refs: final_kernel(scale, *refs),
        out_shape=(shape((owned, LAT), f32), *(shape((h, LAT), f32) for h in heights)),
        in_specs=[
            scalars(),
            scalars(),
            whole(ghost_rows.shape),
            *(whole(x.shape) for x in arrays),
        ],
        compiler_params=params(32),
        cost_estimate=cost(2 * 2048 * 512 * 256, 2 * MIB),
        name="final",
    )(place, ghost_count, ghost_rows, *arrays)


def ring(n, shift):
    return [(i, (i + shift) % n) for i in range(n)]


def body(
    nodes,
    ghost_rows,
    ghost_count,
    edge_send,
    edge_recv,
    edge_count,
    pool_map,
    w_edge_in,
    w_edge_out,
    w_node_in,
    w_node_out,
    w_coarse_in,
    w_coarse_out,
    d_fine,
    d_coarse,
):
    owned = nodes.shape[0]
    slots = ghost_rows.shape[2]
    coarse = d_coarse.shape[0]
    n_gx, n_gy = lax.axis_size(GX), lax.axis_size("gy")
    place = jnp.stack([lax.axis_index(GX), lax.axis_index("gy"), n_gx, n_gy]).astype(jnp.int32)

    out_up, out_down, out_mid, gcol = call_pick(place, ghost_count, ghost_rows, nodes)
    up = lax.ppermute(out_up, GX, ring(n_gx, 1))
    down = lax.ppermute(out_down, GX, ring(n_gx, -1))
    recvs, rcol = call_own(edge_count, edge_recv, nodes)
    up, down, recvs = lax.optimization_barrier((up, down, recvs))

    yup = lax.ppermute(
        jnp.concatenate(
            [up[2 * slots :], out_mid[slots:], down[2 * slots :], d_coarse[coarse - BAND :]]
        ),
        "gy",
        ring(n_gy, 1),
    )
    ydown = lax.ppermute(
        jnp.concatenate([up[:slots], out_mid[:slots], down[:slots], d_coarse[:BAND]]),
        "gy",
        ring(n_gy, -1),
    )
    sown, scol = call_own(edge_count, edge_send, nodes)

    (senders, act, slope, fine_out, summed, nact, nslope, window, wlow, whigh) = call_forward(
        edge_count,
        edge_recv,
        scol,
        rcol,
        sown,
        recvs,
        up,
        down,
        yup,
        ydown,
        nodes,
        pool_map,
        coarse + 2 * BAND,
        w_edge_in,
        w_edge_out,
        w_node_in,
        w_node_out,
    )

    nlow = lax.ppermute(whigh, "gy", ring(n_gy, 1))
    nhigh = lax.ppermute(wlow, "gy", ring(n_gy, -1))

    coarse_out, d_node, d_edge, grads = call_backward(
        (rcol, senders, recvs, act, slope),
        (
            window,
            nlow,
            nhigh,
            yup[3 * slots :],
            ydown[3 * slots :],
            d_coarse,
            d_fine,
            pool_map,
            nodes,
            summed,
            nact,
            nslope,
            w_edge_in,
            w_edge_out,
            w_node_in,
            w_node_out,
            w_coarse_in,
            w_coarse_out,
        ),
    )
    r_down, r_up, r_own = call_ghost(edge_count, edge_send, scol, d_edge, w_edge_in, owned, slots)
    high = lax.ppermute(r_down, "gy", ring(n_gy, -1))
    low = lax.ppermute(r_up, "gy", ring(n_gy, 1))
    d_own = call_local(
        edge_count, edge_send, edge_recv, scol, rcol, d_edge, d_node, w_edge_in
    )
    high, low, d_own = lax.optimization_barrier((high, low, d_own))

    ret_up = lax.ppermute(
        jnp.concatenate([low[:slots], r_own[slots:], high[:slots]]), GX, ring(n_gx, -1)
    )
    ret_down = lax.ppermute(
        jnp.concatenate([low[2 * slots :], r_own[:slots], high[2 * slots :]]), GX, ring(n_gx, 1)
    )

    sums = reduced(grads)
    grad_scale = 1.0 / (owned * n_gx * n_gy) ** 0.5
    grad_nodes, *scaled = call_final(
        grad_scale, place, ghost_count, ghost_rows, gcol, ret_down, ret_up, low, high, d_own, sums
    )
    return (fine_out, coarse_out, grad_nodes, *scaled)


def solution(mesh):
    torus = Mesh(mesh.devices.reshape(4, 4, 2, mesh.shape["gy"]), GX_GY)
    in_specs = (
        P(GX_GY, None),
        P(GX_GY, None, None),
        P(GX_GY, None),
        P(GX_GY, None),
        P(GX_GY, None),
        P(GX_GY),
        P(GX_GY, None),
        P(),
        P(),
        P(),
        P(),
        P(),
        P(),
        P(GX_GY, None),
        P(GX_GY, None),
    )
    out_specs = (P(GX_GY, None), P(GX_GY, None), P(GX_GY, None), P(), P(), P(), P(), P(), P())
    return jax.shard_map(body, mesh=torus, in_specs=in_specs, out_specs=out_specs, check_vma=False)
```

```python
import jax
import jax.numpy as jnp
from jax import lax
from jax.experimental import pallas as pl
from jax.experimental.pallas import tpu as pltpu
from jax.sharding import Mesh
from jax.sharding import PartitionSpec as P

BAND = 32
LAT = 128
LOW = 512
BITS = 9
CHUNK = 1024
FWD_CHUNK = 4096
FWD_MIB = BWD_MIB = 24
GX_GY = ("gx_0", "gx_1", "gx_2", "gy")
GX = ("gx_0", "gx_1", "gx_2")
ACROSS = (-1, -1, -1, 0, 0, 1, 1, 1)
ALONG = (-1, 0, 1, -1, 1, -1, 0, 1)
MIB = 1024 * 1024

f32 = jnp.float32
bf16 = jnp.bfloat16


def mm(left, right):
    return jnp.dot(left, right, preferred_element_type=f32)


def mm_nt(left, right):
    return lax.dot_general(left, right, (((1,), (1,)), ((), ())), preferred_element_type=f32)


def mm_tn(left, right):
    return lax.dot_general(left, right, (((0,), (0,)), ((), ())), preferred_element_type=f32)


def wide(table):
    groups = table.shape[0] // LOW
    return jnp.concatenate([table[i * LOW : (i + 1) * LOW] for i in range(groups)], axis=1)


def tall(table):
    groups = table.shape[1] // LAT
    return jnp.concatenate([table[:, i * LAT : (i + 1) * LAT] for i in range(groups)], axis=0)


def in_columns(row):
    parts = []
    for j in range(row.shape[1] // LAT):
        parts.append(jnp.broadcast_to(row[:, j * LAT : (j + 1) * LAT], (LAT, LAT)).T)
    return jnp.concatenate(parts, axis=0).astype(jnp.int16)


def one_hot(col, rows):
    lanes = lax.broadcasted_iota(jnp.int16, col.shape, 1)
    one, zero = jnp.ones((), bf16), jnp.zeros((), bf16)
    return jnp.concatenate(
        [jnp.where(col == lanes + j * LAT, one, zero) for j in range(rows // LAT)], axis=1
    )


def one_hot_t(row, rows):
    ids = lax.broadcasted_iota(jnp.int16, (rows, row.shape[1]), 0)
    col = jnp.broadcast_to(row, (16, row.shape[1])).astype(jnp.int16)
    col = jnp.concatenate([col] * (rows // 16), axis=0)
    return jnp.where(ids == col, jnp.ones((), bf16), jnp.zeros((), bf16))


def take(col, table):
    got = mm(one_hot(col & (LOW - 1), LOW), table).astype(bf16)
    group = col >> BITS
    total = jnp.zeros((col.shape[0], LAT), bf16)
    for i in range(table.shape[1] // LAT):
        total = jnp.where(group == i, got[:, i * LAT : (i + 1) * LAT], total)
    return total


def put(row, col, values, groups):
    group = col >> BITS
    zero = jnp.zeros((), bf16)
    spread = jnp.concatenate([jnp.where(group == i, values, zero) for i in range(groups)], axis=1)
    return mm(one_hot_t(row & (LOW - 1), LOW), spread)


def sigmoid(v):
    return 0.5 + 0.5 * jnp.tanh(0.5 * v)


def act_and_slope(v):
    s = sigmoid(v)
    return v * s, s * (1.0 + v * (1.0 - s))


def live_row(row, first, count):
    ids = lax.broadcasted_iota(jnp.int32, row.shape, 1) + first
    return jnp.where(ids < count, row, -1)


def live_slots(place_ref, count_ref, k):
    a = place_ref[0] + ACROSS[k]
    b = place_ref[1] + ALONG[k]
    inside = (a >= 0) & (a < place_ref[2]) & (b >= 0) & (b < place_ref[3])
    return jnp.where(inside, count_ref[0, k], 0)


def pick_kernel(place_ref, count_ref, rows_hbm, nodes_hbm, up_ref, down_ref, mid_ref, cols_ref, rows, nodes, sems):
    copies = (
        pltpu.make_async_copy(nodes_hbm, nodes, sems.at[0]),
        pltpu.make_async_copy(rows_hbm, rows, sems.at[1]),
    )
    for copy in copies:
        copy.start()
    for copy in copies:
        copy.wait()
    table = wide(nodes[...])
    slots = rows.shape[2]
    for k in range(8):
        row = live_row(rows[0, k : k + 1, :], 0, live_slots(place_ref, count_ref, k))
        col = in_columns(row)
        cols_ref[k * slots : (k + 1) * slots, :] = col
        got = take(col, table)
        if k < 3:
            down_ref[k * slots : (k + 1) * slots, :] = got
        elif k < 5:
            mid_ref[(k - 3) * slots : (k - 2) * slots, :] = got
        else:
            up_ref[(k - 5) * slots : (k - 4) * slots, :] = got


def own_kernel(count_ref, index_ref, nodes_ref, out_ref, cols_ref):
    table = wide(nodes_ref[...])
    col = in_columns(live_row(index_ref[...], 0, count_ref[0]))
    cols_ref[...] = col
    out_ref[...] = take(col, table)


def forward_kernel(
    count_ref,
    recv_ref,
    scol_ref,
    rcol_ref,
    sown_ref,
    recvs_ref,
    up_ref,
    down_ref,
    yup_ref,
    ydown_ref,
    nodes_ref,
    pool_ref,
    wei_ref,
    weo_ref,
    wni_ref,
    wno_ref,
    senders_ref,
    act_ref,
    slope_ref,
    fine_ref,
    summed_ref,
    nact_ref,
    nslope_ref,
    window_ref,
    wlow_ref,
    whigh_ref,
    table,
    message,
):
    slots = up_ref.shape[0] // 3

    def block(ref, i):
        return ref[i * slots : (i + 1) * slots, :]

    blocks = (
        block(ydown_ref, 2),
        block(down_ref, 1),
        block(yup_ref, 2),
        block(ydown_ref, 1),
        block(yup_ref, 1),
        block(ydown_ref, 0),
        block(up_ref, 1),
        block(yup_ref, 0),
    )
    for k in range(8):
        table[(k % 2) * slots : (k % 2 + 1) * slots, (k // 2) * LAT : (k // 2 + 1) * LAT] = blocks[k]

    owned = nodes_ref.shape[0]
    edges = recv_ref.shape[1]
    for first in range(0, edges, FWD_CHUNK):
        here = slice(first, first + FWD_CHUNK)
        senders = take(scol_ref[here, :] - owned, table[...]) + sown_ref[here, :]
        senders_ref[here, :] = senders
        pre = mm(jnp.concatenate([senders, recvs_ref[here, :]], axis=1), wei_ref[...])
        act, slope = act_and_slope(pre)
        act = act.astype(bf16)
        act_ref[here, :] = act
        slope_ref[here, :] = slope.astype(bf16)
        message[here, :] = mm(act, weo_ref[...]).astype(bf16)
    recv = live_row(recv_ref[...], 0, count_ref[0])
    summed = tall(put(recv, rcol_ref[...], message[...], owned // LOW)).astype(bf16)
    summed_ref[...] = summed
    nodes = nodes_ref[...]
    pre = mm(jnp.concatenate([nodes, summed], axis=1), wni_ref[...])
    act, slope = act_and_slope(pre)
    act = act.astype(bf16)
    nact_ref[...] = act
    nslope_ref[...] = slope.astype(bf16)
    fine = (nodes.astype(f32) + mm(act, wno_ref[...])).astype(bf16)
    fine_ref[...] = fine
    rows = window_ref.shape[0]
    window = mm(one_hot_t(pool_ref[...], rows), fine)
    window_ref[...] = window
    wlow_ref[...] = window[: 2 * BAND].astype(bf16)
    whigh_ref[...] = window[rows - 2 * BAND :].astype(bf16)


def backward_kernel(
    rcol_ref,
    senders_ref,
    recvs_ref,
    act_ref,
    slope_ref,
    window_ref,
    nlow_ref,
    nhigh_ref,
    dcl_ref,
    dch_ref,
    dcoarse_ref,
    dfine_ref,
    pool_ref,
    nodes_ref,
    summed_ref,
    nact_ref,
    nslope_ref,
    wei_ref,
    weo_ref,
    wni_ref,
    wno_ref,
    wci_ref,
    wco_ref,
    coarse_ref,
    dnode_ref,
    dedge_ref,
    grads_ref,
    table,
):
    window = window_ref[...]
    rows = window.shape[0]
    total = jnp.concatenate(
        [
            window[: 2 * BAND] + nlow_ref[...].astype(f32),
            window[2 * BAND : rows - 2 * BAND],
            window[rows - 2 * BAND :] + nhigh_ref[...].astype(f32),
        ],
        axis=0,
    )
    coarse_in = (0.125 * total).astype(bf16)
    d_coarse = jnp.concatenate([dcl_ref[...], dcoarse_ref[...], dch_ref[...]], axis=0)
    act, slope = act_and_slope(mm(coarse_in, wci_ref[...]))
    act = act.astype(bf16)
    coarse_out = (coarse_in.astype(f32) + mm(act, wco_ref[...])).astype(bf16)
    coarse_ref[...] = coarse_out[BAND : rows - BAND]
    d_pre = (mm_nt(d_coarse, wco_ref[...]) * slope).astype(bf16)
    d_in = (d_coarse.astype(f32) + mm_nt(d_pre, wci_ref[...])).astype(bf16)
    inner = slice(BAND, rows - BAND)
    g_ci = mm_tn(coarse_in[inner], d_pre[inner])
    g_co = mm_tn(act[inner], d_coarse[inner])
    reach = jnp.concatenate([d_in, jnp.zeros((2 * LAT - rows, LAT), bf16)], axis=0)
    parent = mm(one_hot(in_columns(pool_ref[...]), 2 * LAT), reach)
    d_total = dfine_ref[...].astype(f32) + 0.125 * parent
    d_out = d_total.astype(bf16)
    d_node = (mm_nt(d_out, wno_ref[...]) * nslope_ref[...].astype(f32)).astype(bf16)
    back = mm_nt(d_node, wni_ref[...])
    dnode_ref[...] = d_total + back[:, :LAT]
    table[...] = wide(back[:, LAT:].astype(bf16))
    g_ni = mm_tn(jnp.concatenate([nodes_ref[...], summed_ref[...]], axis=1), d_node)
    g_no = mm_tn(nact_ref[...], d_out)
    grads_ref[3 * LAT : 5 * LAT, :] = g_ni.astype(bf16)
    grads_ref[5 * LAT : 6 * LAT, :] = g_no.astype(bf16)
    grads_ref[6 * LAT : 7 * LAT, :] = g_ci.astype(bf16)
    grads_ref[7 * LAT :, :] = g_co.astype(bf16)

    edges = rcol_ref.shape[0]
    g_ei = jnp.zeros((2 * LAT, LAT), f32)
    g_eo = jnp.zeros((LAT, LAT), f32)
    for first in range(0, edges, CHUNK):
        here = slice(first, first + CHUNK)
        d_message = take(rcol_ref[here, :], table[...])
        d_pre = (mm_nt(d_message, weo_ref[...]) * slope_ref[here, :].astype(f32)).astype(bf16)
        dedge_ref[here, :] = d_pre
        ends = jnp.concatenate([senders_ref[here, :], recvs_ref[here, :]], axis=1)
        g_ei = g_ei + mm_tn(ends, d_pre)
        g_eo = g_eo + mm_tn(act_ref[here, :], d_message)
    grads_ref[: 2 * LAT, :] = g_ei.astype(bf16)
    grads_ref[2 * LAT : 3 * LAT, :] = g_eo.astype(bf16)


def ghost_kernel(count_ref, send_ref, dedge_ref, wei_ref, rdown_ref, rup_ref, rown_ref, *, owned):
    send = live_row(send_ref[...], 0, count_ref[0]) - owned
    total = put(send, in_columns(send), dedge_ref[...], 4)
    ghosts = mm_nt(tall(total).astype(bf16), wei_ref[:LAT, :]).astype(bf16)
    slots = ghosts.shape[0] // 8
    for place, (ref, i) in enumerate(
        (
            (rup_ref, 2),
            (rown_ref, 0),
            (rdown_ref, 2),
            (rup_ref, 1),
            (rdown_ref, 1),
            (rup_ref, 0),
            (rown_ref, 1),
            (rdown_ref, 0),
        )
    ):
        ref[i * slots : (i + 1) * slots, :] = ghosts[place * slots : (place + 1) * slots]


def local_kernel(count_ref, send_ref, recv_ref, dedge_ref, dnode_ref, wei_ref, out_ref):
    groups = out_ref.shape[0] // LOW
    d_pre = dedge_ref[...]
    send = live_row(send_ref[...], 0, count_ref[0])
    recv = live_row(recv_ref[...], 0, count_ref[0])
    by_send = tall(put(send, in_columns(send), d_pre, groups)).astype(bf16)
    by_recv = tall(put(recv, in_columns(recv), d_pre, groups)).astype(bf16)
    out_ref[...] = dnode_ref[...] + mm_nt(
        jnp.concatenate([by_send, by_recv], axis=1),
        jnp.concatenate([wei_ref[:LAT, :], wei_ref[LAT:, :]], axis=1),
    )


def return_kernel(
    place_ref,
    count_ref,
    rows_ref,
    cols_ref,
    down_ref,
    up_ref,
    mid_low_ref,
    mid_high_ref,
    part_ref,
    out_ref,
):
    slots = rows_ref.shape[2]
    groups = out_ref.shape[0] // LOW
    total = jnp.zeros((LOW, groups * LAT), f32)
    for k in range(8):
        row = live_row(rows_ref[0, k : k + 1, :], 0, live_slots(place_ref, count_ref, k))
        col = cols_ref[k * slots : (k + 1) * slots, :]
        if k < 3:
            got = down_ref[k * slots : (k + 1) * slots, :]
        elif k == 3:
            got = mid_low_ref[slots : 2 * slots, :]
        elif k == 4:
            got = mid_high_ref[slots : 2 * slots, :]
        else:
            got = up_ref[(k - 5) * slots : (k - 4) * slots, :]
        total = total + put(row, col, got, groups)
    out_ref[...] = part_ref[...] + tall(total)


def scale_kernel(scale, sums_ref, *grad_refs):
    first = 0
    for ref in grad_refs:
        rows = ref.shape[0]
        ref[...] = sums_ref[first : first + rows, :].astype(f32) * scale
        first += rows


def scalars():
    return pl.BlockSpec(memory_space=pltpu.SMEM)


def inside(count):
    return [pl.BlockSpec(memory_space=pltpu.VMEM)] * count


def hbm():
    return pl.BlockSpec(memory_space=pltpu.HBM)


def shape(dims, dtype):
    return jax.ShapeDtypeStruct(dims, dtype)


def params(mib):
    return pltpu.CompilerParams(vmem_limit_bytes=mib * MIB)


def cost(flops, moved):
    return pl.CostEstimate(flops=flops, bytes_accessed=moved, transcendentals=0)


def scattered(grads):
    n_far = lax.axis_size(GX)
    got = lax.all_to_all(grads.reshape(n_far, -1, LAT), GX, 0, 0, tiled=True)
    return got.astype(f32).sum(axis=0).astype(bf16)


def to_all(own, axis):
    pieces = jnp.broadcast_to(own[None], (lax.axis_size(axis), *own.shape))
    return lax.all_to_all(pieces, axis, 0, 0, tiled=True)


def call_pick(place, ghost_count, ghost_rows, nodes):
    slots = ghost_rows.shape[2]
    return pl.pallas_call(
        pick_kernel,
        out_shape=(
            shape((3 * slots, LAT), bf16),
            shape((3 * slots, LAT), bf16),
            shape((2 * slots, LAT), bf16),
            shape((8 * slots, LAT), jnp.int16),
        ),
        in_specs=[scalars(), scalars(), hbm(), hbm()],
        out_specs=tuple(inside(4)),
        scratch_shapes=[
            pltpu.VMEM(ghost_rows.shape, jnp.int32),
            pltpu.VMEM(nodes.shape, bf16),
            pltpu.SemaphoreType.DMA((2,)),
        ],
        compiler_params=params(32),
        cost_estimate=cost(2 * 2048 * 512 * 256, MIB),
        name="pick",
    )(place, ghost_count, ghost_rows, nodes)


def call_own(edge_count, index, nodes):
    edges = index.shape[1]
    return pl.pallas_call(
        own_kernel,
        out_shape=(shape((edges, LAT), bf16), shape((edges, LAT), jnp.int16)),
        in_specs=[scalars(), *inside(2)],
        out_specs=tuple(inside(2)),
        compiler_params=params(24),
        cost_estimate=cost(2 * 4096 * 512 * 256, 2 * MIB),
        name="own_rows",
    )(edge_count, index, nodes)


def call_forward(edge_count, recv, rows, *plain):
    edges, owned = recv.shape[1], plain[8].shape[0]
    edge16 = shape((edges, LAT), bf16)
    node16 = shape((owned, LAT), bf16)
    band = shape((2 * BAND, LAT), bf16)
    outs = (edge16,) * 3 + (node16,) * 4 + (shape((rows, LAT), f32), band, band)
    return pl.pallas_call(
        forward_kernel,
        out_shape=outs,
        in_specs=[scalars(), *inside(1 + len(plain))],
        out_specs=tuple(inside(len(outs))),
        scratch_shapes=[pltpu.VMEM((LOW, 4 * LAT), bf16), pltpu.VMEM((edges, LAT), bf16)],
        compiler_params=params(FWD_MIB),
        cost_estimate=cost(2 * 4096 * 512 * 1024, 8 * MIB),
        name="forward",
    )(edge_count, recv, *plain)


def call_backward(edge_arrays, plain):
    edges = edge_arrays[0].shape[0]
    owned, coarse = plain[8].shape[0], plain[5].shape[0]
    return pl.pallas_call(
        backward_kernel,
        out_shape=(
            shape((coarse, LAT), bf16),
            shape((owned, LAT), f32),
            shape((edges, LAT), bf16),
            shape((8 * LAT, LAT), bf16),
        ),
        in_specs=inside(len(edge_arrays) + len(plain)),
        out_specs=tuple(inside(4)),
        scratch_shapes=[pltpu.VMEM((LOW, owned // LOW * LAT), bf16)],
        compiler_params=params(BWD_MIB),
        cost_estimate=cost(2 * 4096 * 512 * 512, 8 * MIB),
        name="backward",
    )(*edge_arrays, *plain)


def call_ghost(edge_count, send, d_edge, w_edge_in, owned, slots):
    return pl.pallas_call(
        lambda *refs: ghost_kernel(*refs, owned=owned),
        out_shape=(
            shape((3 * slots, LAT), bf16),
            shape((3 * slots, LAT), bf16),
            shape((2 * slots, LAT), bf16),
        ),
        in_specs=[scalars(), *inside(3)],
        out_specs=tuple(inside(3)),
        compiler_params=params(24),
        cost_estimate=cost(2 * 4096 * 512 * 512, 3 * MIB),
        name="ghost_grads",
    )(edge_count, send, d_edge, w_edge_in)


def call_local(edge_count, send, recv, d_edge, d_node, w_edge_in):
    return pl.pallas_call(
        local_kernel,
        out_shape=shape(d_node.shape, f32),
        in_specs=[scalars(), *inside(5)],
        out_specs=inside(1)[0],
        compiler_params=params(24),
        cost_estimate=cost(2 * 2 * 4096 * 512 * 256, 3 * MIB),
        name="local",
    )(edge_count, send, recv, d_edge, d_node, w_edge_in)


def call_return(place, ghost_count, *arrays):
    owned = arrays[-1].shape[0]
    return pl.pallas_call(
        return_kernel,
        out_shape=shape((owned, LAT), f32),
        in_specs=[scalars(), scalars(), *inside(len(arrays))],
        out_specs=inside(1)[0],
        compiler_params=params(24),
        cost_estimate=cost(2 * 2048 * 512 * 256, 2 * MIB),
        name="returned",
    )(place, ghost_count, *arrays)


def call_scale(scale, sums):
    heights = (2 * LAT, LAT, 2 * LAT, LAT, LAT, LAT)
    return pl.pallas_call(
        lambda *refs: scale_kernel(scale, *refs),
        out_shape=tuple(shape((h, LAT), f32) for h in heights),
        in_specs=inside(1),
        out_specs=tuple(inside(6)),
        compiler_params=params(8),
        name="scaled",
    )(sums)


def ring(n, shift):
    return [(i, (i + shift) % n) for i in range(n)]


def body(
    nodes,
    ghost_rows,
    ghost_count,
    edge_send,
    edge_recv,
    edge_count,
    pool_map,
    w_edge_in,
    w_edge_out,
    w_node_in,
    w_node_out,
    w_coarse_in,
    w_coarse_out,
    d_fine,
    d_coarse,
):
    owned = nodes.shape[0]
    slots = ghost_rows.shape[2]
    coarse = d_coarse.shape[0]
    n_gx, n_gy = lax.axis_size(GX), lax.axis_size("gy")
    place = jnp.stack([lax.axis_index(GX), lax.axis_index("gy"), n_gx, n_gy]).astype(jnp.int32)

    out_up, out_down, out_mid, gcol = call_pick(place, ghost_count, ghost_rows, nodes)
    up = lax.ppermute(out_up, GX, ring(n_gx, 1))
    down = lax.ppermute(out_down, GX, ring(n_gx, -1))
    recvs, rcol = call_own(edge_count, edge_recv, nodes)
    up, down, recvs = lax.optimization_barrier((up, down, recvs))

    yup = lax.ppermute(
        jnp.concatenate(
            [up[2 * slots :], out_mid[slots:], down[2 * slots :], d_coarse[coarse - BAND :]]
        ),
        "gy",
        ring(n_gy, 1),
    )
    ydown = lax.ppermute(
        jnp.concatenate([up[:slots], out_mid[:slots], down[:slots], d_coarse[:BAND]]),
        "gy",
        ring(n_gy, -1),
    )
    sown, scol = call_own(edge_count, edge_send, nodes)

    (senders, act, slope, fine_out, summed, nact, nslope, window, wlow, whigh) = call_forward(
        edge_count,
        edge_recv,
        coarse + 2 * BAND,
        scol,
        rcol,
        sown,
        recvs,
        up,
        down,
        yup,
        ydown,
        nodes,
        pool_map,
        w_edge_in,
        w_edge_out,
        w_node_in,
        w_node_out,
    )

    nlow = lax.ppermute(whigh, "gy", ring(n_gy, 1))
    nhigh = lax.ppermute(wlow, "gy", ring(n_gy, -1))

    coarse_out, d_node, d_edge, grads = call_backward(
        (rcol, senders, recvs, act, slope),
        (
            window,
            nlow,
            nhigh,
            yup[3 * slots :],
            ydown[3 * slots :],
            d_coarse,
            d_fine,
            pool_map,
            nodes,
            summed,
            nact,
            nslope,
            w_edge_in,
            w_edge_out,
            w_node_in,
            w_node_out,
            w_coarse_in,
            w_coarse_out,
        ),
    )
    r_down, r_up, r_own = call_ghost(edge_count, edge_send, d_edge, w_edge_in, owned, slots)
    high = lax.ppermute(r_down, "gy", ring(n_gy, -1))
    low = lax.ppermute(r_up, "gy", ring(n_gy, 1))
    d_own = call_local(edge_count, edge_send, edge_recv, d_edge, d_node, w_edge_in)
    high, low, d_own = lax.optimization_barrier((high, low, d_own))

    ret_up = lax.ppermute(
        jnp.concatenate([low[:slots], r_own[slots:], high[:slots]]), GX, ring(n_gx, -1)
    )
    ret_down = lax.ppermute(
        jnp.concatenate([low[2 * slots :], r_own[:slots], high[2 * slots :]]), GX, ring(n_gx, 1)
    )

    own = scattered(grads)
    own = to_all(own, "gy").astype(f32).sum(axis=0).astype(bf16)
    own, ret_down, ret_up = lax.optimization_barrier((own, ret_down, ret_up))
    sums = to_all(own, GX).reshape(grads.shape)
    grad_nodes = call_return(
        place, ghost_count, ghost_rows, gcol, ret_down, ret_up, low, high, d_own
    )
    scaled = call_scale(1.0 / (owned * n_gx * n_gy) ** 0.5, sums)
    return (fine_out, coarse_out, grad_nodes, *scaled)


def solution(mesh):
    torus = Mesh(mesh.devices.reshape(4, 4, 2, mesh.shape["gy"]), GX_GY)
    in_specs = (
        P(GX_GY, None),
        P(GX_GY, None, None),
        P(GX_GY, None),
        P(GX_GY, None),
        P(GX_GY, None),
        P(GX_GY),
        P(GX_GY, None),
        P(),
        P(),
        P(),
        P(),
        P(),
        P(),
        P(GX_GY, None),
        P(GX_GY, None),
    )
    out_specs = (P(GX_GY, None), P(GX_GY, None), P(GX_GY, None), P(), P(), P(), P(), P(), P())
    return jax.shard_map(body, mesh=torus, in_specs=in_specs, out_specs=out_specs, check_vma=False)
```

```python
import jax
import jax.numpy as jnp
from jax import lax
from jax.experimental import pallas as pl
from jax.experimental.pallas import tpu as pltpu
from jax.sharding import Mesh
from jax.sharding import PartitionSpec as P

BAND = 32
LAT = 128
LOW = 512
BITS = 9
CHUNK = 1024
FWD_CHUNK = 4096
FWD_MIB = BWD_MIB = 20
GX_GY = ("gx_0", "gx_1", "gx_2", "gy")
GX = ("gx_0", "gx_1", "gx_2")
ACROSS = (-1, -1, -1, 0, 0, 1, 1, 1)
ALONG = (-1, 0, 1, -1, 1, -1, 0, 1)
MIB = 1024 * 1024

f32 = jnp.float32
bf16 = jnp.bfloat16


def mm(left, right):
    return jnp.dot(left, right, preferred_element_type=f32)


def mm_nt(left, right):
    return lax.dot_general(left, right, (((1,), (1,)), ((), ())), preferred_element_type=f32)


def mm_tn(left, right):
    return lax.dot_general(left, right, (((0,), (0,)), ((), ())), preferred_element_type=f32)


def wide(table):
    groups = table.shape[0] // LOW
    return jnp.concatenate([table[i * LOW : (i + 1) * LOW] for i in range(groups)], axis=1)


def tall(table):
    groups = table.shape[1] // LAT
    return jnp.concatenate([table[:, i * LAT : (i + 1) * LAT] for i in range(groups)], axis=0)


def in_columns(row):
    parts = []
    for j in range(row.shape[1] // LAT):
        parts.append(jnp.broadcast_to(row[:, j * LAT : (j + 1) * LAT], (LAT, LAT)).T)
    return jnp.concatenate(parts, axis=0).astype(jnp.int16)


def one_hot(col, rows):
    lanes = lax.broadcasted_iota(jnp.int16, col.shape, 1)
    one, zero = jnp.ones((), bf16), jnp.zeros((), bf16)
    return jnp.concatenate(
        [jnp.where(col == lanes + j * LAT, one, zero) for j in range(rows // LAT)], axis=1
    )


def one_hot_t(row, rows):
    ids = lax.broadcasted_iota(jnp.int16, (rows, row.shape[1]), 0)
    col = jnp.broadcast_to(row, (16, row.shape[1])).astype(jnp.int16)
    col = jnp.concatenate([col] * (rows // 16), axis=0)
    return jnp.where(ids == col, jnp.ones((), bf16), jnp.zeros((), bf16))


def take(col, table):
    got = mm(one_hot(col & (LOW - 1), LOW), table)
    group = col.astype(jnp.int32) >> BITS
    total = jnp.zeros((col.shape[0], LAT), f32)
    for i in range(table.shape[1] // LAT):
        total = jnp.where(group == i, got[:, i * LAT : (i + 1) * LAT], total)
    return total.astype(bf16)


def put(row, col, values, groups):
    group = col >> BITS
    zero = jnp.zeros((), bf16)
    spread = jnp.concatenate([jnp.where(group == i, values, zero) for i in range(groups)], axis=1)
    return mm(one_hot_t(row & (LOW - 1), LOW), spread)


def sigmoid(v):
    return 0.5 + 0.5 * jnp.tanh(0.5 * v)


def act_and_slope(v):
    s = sigmoid(v)
    return v * s, s * (1.0 + v * (1.0 - s))


def live_row(row, first, count):
    ids = lax.broadcasted_iota(jnp.int32, row.shape, 1) + first
    return jnp.where(ids < count, row, -1)


def live_slots(place_ref, count_ref, k):
    a = place_ref[0] + ACROSS[k]
    b = place_ref[1] + ALONG[k]
    inside = (a >= 0) & (a < place_ref[2]) & (b >= 0) & (b < place_ref[3])
    return jnp.where(inside, count_ref[0, k], 0)


def pick_kernel(place_ref, count_ref, rows_hbm, nodes_hbm, up_ref, down_ref, mid_ref, cols_ref, rows, nodes, sems):
    copies = (
        pltpu.make_async_copy(nodes_hbm, nodes, sems.at[0]),
        pltpu.make_async_copy(rows_hbm, rows, sems.at[1]),
    )
    for copy in copies:
        copy.start()
    for copy in copies:
        copy.wait()
    table = wide(nodes[...])
    slots = rows.shape[2]
    for k in range(8):
        row = live_row(rows[0, k : k + 1, :], 0, live_slots(place_ref, count_ref, k))
        col = in_columns(row)
        cols_ref[k * slots : (k + 1) * slots, :] = col
        got = take(col, table)
        if k < 3:
            down_ref[k * slots : (k + 1) * slots, :] = got
        elif k < 5:
            mid_ref[(k - 3) * slots : (k - 2) * slots, :] = got
        else:
            up_ref[(k - 5) * slots : (k - 4) * slots, :] = got


def own_kernel(count_ref, index_ref, nodes_ref, out_ref, cols_ref):
    table = wide(nodes_ref[...])
    col = in_columns(live_row(index_ref[...], 0, count_ref[0]))
    cols_ref[...] = col
    out_ref[...] = take(col, table)


def forward_kernel(
    count_ref,
    recv_ref,
    scol_ref,
    rcol_ref,
    sown_ref,
    recvs_ref,
    up_ref,
    down_ref,
    yup_ref,
    ydown_ref,
    nodes_ref,
    pool_ref,
    wei_ref,
    weo_ref,
    wni_ref,
    wno_ref,
    senders_ref,
    act_ref,
    slope_ref,
    fine_ref,
    summed_ref,
    nact_ref,
    nslope_ref,
    window_ref,
    wlow_ref,
    whigh_ref,
    table,
    message,
):
    slots = up_ref.shape[0] // 3

    def block(ref, i):
        return ref[i * slots : (i + 1) * slots, :]

    blocks = (
        block(ydown_ref, 2),
        block(down_ref, 1),
        block(yup_ref, 2),
        block(ydown_ref, 1),
        block(yup_ref, 1),
        block(ydown_ref, 0),
        block(up_ref, 1),
        block(yup_ref, 0),
    )
    for k in range(8):
        table[(k % 2) * slots : (k % 2 + 1) * slots, (k // 2) * LAT : (k // 2 + 1) * LAT] = blocks[k]

    owned = nodes_ref.shape[0]
    edges = recv_ref.shape[1]
    for first in range(0, edges, FWD_CHUNK):
        here = slice(first, first + FWD_CHUNK)
        senders = take(scol_ref[here, :] - owned, table[...]) + sown_ref[here, :]
        senders_ref[here, :] = senders
        pre = mm(jnp.concatenate([senders, recvs_ref[here, :]], axis=1), wei_ref[...])
        act, slope = act_and_slope(pre)
        act = act.astype(bf16)
        act_ref[here, :] = act
        slope_ref[here, :] = slope.astype(bf16)
        message[here, :] = mm(act, weo_ref[...]).astype(bf16)
    recv = live_row(recv_ref[...], 0, count_ref[0])
    summed = tall(put(recv, rcol_ref[...], message[...], owned // LOW)).astype(bf16)
    summed_ref[...] = summed
    nodes = nodes_ref[...]
    pre = mm(jnp.concatenate([nodes, summed], axis=1), wni_ref[...])
    act, slope = act_and_slope(pre)
    act = act.astype(bf16)
    nact_ref[...] = act
    nslope_ref[...] = slope.astype(bf16)
    fine = (nodes.astype(f32) + mm(act, wno_ref[...])).astype(bf16)
    fine_ref[...] = fine
    rows = window_ref.shape[0]
    window = mm(one_hot_t(pool_ref[...], rows), fine)
    window_ref[...] = window
    wlow_ref[...] = window[: 2 * BAND].astype(bf16)
    whigh_ref[...] = window[rows - 2 * BAND :].astype(bf16)


def backward_kernel(
    rcol_ref,
    senders_ref,
    recvs_ref,
    act_ref,
    slope_ref,
    window_ref,
    nlow_ref,
    nhigh_ref,
    dcl_ref,
    dch_ref,
    dcoarse_ref,
    dfine_ref,
    pool_ref,
    nodes_ref,
    summed_ref,
    nact_ref,
    nslope_ref,
    wei_ref,
    weo_ref,
    wni_ref,
    wno_ref,
    wci_ref,
    wco_ref,
    coarse_ref,
    dnode_ref,
    dedge_ref,
    grads_ref,
    table,
):
    window = window_ref[...]
    rows = window.shape[0]
    total = jnp.concatenate(
        [
            window[: 2 * BAND] + nlow_ref[...].astype(f32),
            window[2 * BAND : rows - 2 * BAND],
            window[rows - 2 * BAND :] + nhigh_ref[...].astype(f32),
        ],
        axis=0,
    )
    coarse_in = (0.125 * total).astype(bf16)
    d_coarse = jnp.concatenate([dcl_ref[...], dcoarse_ref[...], dch_ref[...]], axis=0)
    act, slope = act_and_slope(mm(coarse_in, wci_ref[...]))
    act = act.astype(bf16)
    coarse_out = (coarse_in.astype(f32) + mm(act, wco_ref[...])).astype(bf16)
    coarse_ref[...] = coarse_out[BAND : rows - BAND]
    d_pre = (mm_nt(d_coarse, wco_ref[...]) * slope).astype(bf16)
    d_in = (d_coarse.astype(f32) + mm_nt(d_pre, wci_ref[...])).astype(bf16)
    inner = slice(BAND, rows - BAND)
    g_ci = mm_tn(coarse_in[inner], d_pre[inner])
    g_co = mm_tn(act[inner], d_coarse[inner])
    reach = jnp.concatenate([d_in, jnp.zeros((2 * LAT - rows, LAT), bf16)], axis=0)
    parent = mm(one_hot(in_columns(pool_ref[...]), 2 * LAT), reach)
    d_total = dfine_ref[...].astype(f32) + 0.125 * parent
    d_out = d_total.astype(bf16)
    d_node = (mm_nt(d_out, wno_ref[...]) * nslope_ref[...].astype(f32)).astype(bf16)
    back = mm_nt(d_node, wni_ref[...])
    dnode_ref[...] = d_total + back[:, :LAT]
    table[...] = wide(back[:, LAT:].astype(bf16))
    g_ni = mm_tn(jnp.concatenate([nodes_ref[...], summed_ref[...]], axis=1), d_node)
    g_no = mm_tn(nact_ref[...], d_out)
    grads_ref[3 * LAT : 5 * LAT, :] = g_ni.astype(bf16)
    grads_ref[5 * LAT : 6 * LAT, :] = g_no.astype(bf16)
    grads_ref[6 * LAT : 7 * LAT, :] = g_ci.astype(bf16)
    grads_ref[7 * LAT :, :] = g_co.astype(bf16)

    edges = rcol_ref.shape[0]
    g_ei = jnp.zeros((2 * LAT, LAT), f32)
    g_eo = jnp.zeros((LAT, LAT), f32)
    for first in range(0, edges, CHUNK):
        here = slice(first, first + CHUNK)
        d_message = take(rcol_ref[here, :], table[...])
        d_pre = (mm_nt(d_message, weo_ref[...]) * slope_ref[here, :].astype(f32)).astype(bf16)
        dedge_ref[here, :] = d_pre
        ends = jnp.concatenate([senders_ref[here, :], recvs_ref[here, :], act_ref[here, :]], axis=1)
        both = mm_tn(ends, jnp.concatenate([d_pre, d_message], axis=1))
        g_ei = g_ei + both[: 2 * LAT, :LAT]
        g_eo = g_eo + both[2 * LAT :, LAT:]
    grads_ref[: 2 * LAT, :] = g_ei.astype(bf16)
    grads_ref[2 * LAT : 3 * LAT, :] = g_eo.astype(bf16)


def ghost_kernel(count_ref, send_ref, dedge_ref, wei_ref, rdown_ref, rup_ref, rown_ref, *, owned):
    send = live_row(send_ref[...], 0, count_ref[0]) - owned
    total = put(send, in_columns(send), dedge_ref[...], 4)
    ghosts = mm_nt(tall(total).astype(bf16), wei_ref[:LAT, :]).astype(bf16)
    slots = ghosts.shape[0] // 8
    for place, (ref, i) in enumerate(
        (
            (rup_ref, 2),
            (rown_ref, 0),
            (rdown_ref, 2),
            (rup_ref, 1),
            (rdown_ref, 1),
            (rup_ref, 0),
            (rown_ref, 1),
            (rdown_ref, 0),
        )
    ):
        ref[i * slots : (i + 1) * slots, :] = ghosts[place * slots : (place + 1) * slots]


def local_kernel(count_ref, send_ref, recv_ref, dedge_ref, dnode_ref, wei_ref, out_ref):
    groups = out_ref.shape[0] // LOW
    d_pre = dedge_ref[...]
    send = live_row(send_ref[...], 0, count_ref[0])
    recv = live_row(recv_ref[...], 0, count_ref[0])
    by_send = tall(put(send, in_columns(send), d_pre, groups)).astype(bf16)
    by_recv = tall(put(recv, in_columns(recv), d_pre, groups)).astype(bf16)
    out_ref[...] = dnode_ref[...] + mm_nt(
        jnp.concatenate([by_send, by_recv], axis=1),
        jnp.concatenate([wei_ref[:LAT, :], wei_ref[LAT:, :]], axis=1),
    )


def return_kernel(
    place_ref,
    count_ref,
    rows_ref,
    cols_ref,
    down_ref,
    up_ref,
    mid_low_ref,
    mid_high_ref,
    part_ref,
    out_ref,
):
    slots = rows_ref.shape[2]
    groups = out_ref.shape[0] // LOW
    total = jnp.zeros((LOW, groups * LAT), f32)
    for k in range(8):
        row = live_row(rows_ref[0, k : k + 1, :], 0, live_slots(place_ref, count_ref, k))
        col = cols_ref[k * slots : (k + 1) * slots, :]
        if k < 3:
            got = down_ref[k * slots : (k + 1) * slots, :]
        elif k == 3:
            got = mid_low_ref[slots : 2 * slots, :]
        elif k == 4:
            got = mid_high_ref[slots : 2 * slots, :]
        else:
            got = up_ref[(k - 5) * slots : (k - 4) * slots, :]
        total = total + put(row, col, got, groups)
    out_ref[...] = part_ref[...] + tall(total)


def scale_kernel(scale, sums_ref, *grad_refs):
    first = 0
    for ref in grad_refs:
        rows = ref.shape[0]
        ref[...] = sums_ref[first : first + rows, :].astype(f32) * scale
        first += rows


def scalars():
    return pl.BlockSpec(memory_space=pltpu.SMEM)


def inside(count):
    return [pl.BlockSpec(memory_space=pltpu.VMEM)] * count


def hbm():
    return pl.BlockSpec(memory_space=pltpu.HBM)


def shape(dims, dtype):
    return jax.ShapeDtypeStruct(dims, dtype)


def params(mib):
    return pltpu.CompilerParams(vmem_limit_bytes=mib * MIB)


def cost(flops, moved):
    return pl.CostEstimate(flops=flops, bytes_accessed=moved, transcendentals=0)


def scattered(grads):
    n_far = lax.axis_size(GX)
    got = lax.all_to_all(grads.reshape(n_far, -1, LAT), GX, 0, 0, tiled=True)
    return got.astype(f32).sum(axis=0).astype(bf16)


def to_all(own, axis):
    pieces = jnp.broadcast_to(own[None], (lax.axis_size(axis), *own.shape))
    return lax.all_to_all(pieces, axis, 0, 0, tiled=True)


def call_pick(place, ghost_count, ghost_rows, nodes):
    slots = ghost_rows.shape[2]
    return pl.pallas_call(
        pick_kernel,
        out_shape=(
            shape((3 * slots, LAT), bf16),
            shape((3 * slots, LAT), bf16),
            shape((2 * slots, LAT), bf16),
            shape((8 * slots, LAT), jnp.int16),
        ),
        in_specs=[scalars(), scalars(), hbm(), hbm()],
        out_specs=tuple(inside(4)),
        scratch_shapes=[
            pltpu.VMEM(ghost_rows.shape, jnp.int32),
            pltpu.VMEM(nodes.shape, bf16),
            pltpu.SemaphoreType.DMA((2,)),
        ],
        compiler_params=params(32),
        cost_estimate=cost(2 * 2048 * 512 * 256, MIB),
        name="pick",
    )(place, ghost_count, ghost_rows, nodes)


def call_own(edge_count, index, nodes):
    edges = index.shape[1]
    return pl.pallas_call(
        own_kernel,
        out_shape=(shape((edges, LAT), bf16), shape((edges, LAT), jnp.int16)),
        in_specs=[scalars(), *inside(2)],
        out_specs=tuple(inside(2)),
        compiler_params=params(16),
        cost_estimate=cost(2 * 4096 * 512 * 256, 2 * MIB),
        name="own_rows",
    )(edge_count, index, nodes)


def call_forward(edge_count, recv, rows, *plain):
    edges, owned = recv.shape[1], plain[8].shape[0]
    edge16 = shape((edges, LAT), bf16)
    node16 = shape((owned, LAT), bf16)
    band = shape((2 * BAND, LAT), bf16)
    outs = (edge16,) * 3 + (node16,) * 4 + (shape((rows, LAT), f32), band, band)
    return pl.pallas_call(
        forward_kernel,
        out_shape=outs,
        in_specs=[scalars(), *inside(1 + len(plain))],
        out_specs=tuple(inside(len(outs))),
        scratch_shapes=[pltpu.VMEM((LOW, 4 * LAT), bf16), pltpu.VMEM((edges, LAT), bf16)],
        compiler_params=params(FWD_MIB),
        cost_estimate=cost(2 * 4096 * 512 * 1024, 8 * MIB),
        name="forward",
    )(edge_count, recv, *plain)


def call_backward(edge_arrays, plain):
    edges = edge_arrays[0].shape[0]
    owned, coarse = plain[8].shape[0], plain[5].shape[0]
    return pl.pallas_call(
        backward_kernel,
        out_shape=(
            shape((coarse, LAT), bf16),
            shape((owned, LAT), f32),
            shape((edges, LAT), bf16),
            shape((8 * LAT, LAT), bf16),
        ),
        in_specs=inside(len(edge_arrays) + len(plain)),
        out_specs=tuple(inside(4)),
        scratch_shapes=[pltpu.VMEM((LOW, owned // LOW * LAT), bf16)],
        compiler_params=params(BWD_MIB),
        cost_estimate=cost(2 * 4096 * 512 * 512, 8 * MIB),
        name="backward",
    )(*edge_arrays, *plain)


def call_ghost(edge_count, send, d_edge, w_edge_in, owned, slots):
    return pl.pallas_call(
        lambda *refs: ghost_kernel(*refs, owned=owned),
        out_shape=(
            shape((3 * slots, LAT), bf16),
            shape((3 * slots, LAT), bf16),
            shape((2 * slots, LAT), bf16),
        ),
        in_specs=[scalars(), *inside(3)],
        out_specs=tuple(inside(3)),
        compiler_params=params(16),
        cost_estimate=cost(2 * 4096 * 512 * 512, 3 * MIB),
        name="ghost_grads",
    )(edge_count, send, d_edge, w_edge_in)


def call_local(edge_count, send, recv, d_edge, d_node, w_edge_in):
    return pl.pallas_call(
        local_kernel,
        out_shape=shape(d_node.shape, f32),
        in_specs=[scalars(), *inside(5)],
        out_specs=inside(1)[0],
        compiler_params=params(16),
        cost_estimate=cost(2 * 2 * 4096 * 512 * 256, 3 * MIB),
        name="local",
    )(edge_count, send, recv, d_edge, d_node, w_edge_in)


def call_return(place, ghost_count, *arrays):
    owned = arrays[-1].shape[0]
    return pl.pallas_call(
        return_kernel,
        out_shape=shape((owned, LAT), f32),
        in_specs=[scalars(), scalars(), *inside(len(arrays))],
        out_specs=inside(1)[0],
        compiler_params=params(16),
        cost_estimate=cost(2 * 2048 * 512 * 256, 2 * MIB),
        name="returned",
    )(place, ghost_count, *arrays)


def call_scale(scale, sums):
    heights = (2 * LAT, LAT, 2 * LAT, LAT, LAT, LAT)
    return pl.pallas_call(
        lambda *refs: scale_kernel(scale, *refs),
        out_shape=tuple(shape((h, LAT), f32) for h in heights),
        in_specs=inside(1),
        out_specs=tuple(inside(6)),
        compiler_params=params(8),
        name="scaled",
    )(sums)


def ring(n, shift):
    return [(i, (i + shift) % n) for i in range(n)]


def body(
    nodes,
    ghost_rows,
    ghost_count,
    edge_send,
    edge_recv,
    edge_count,
    pool_map,
    w_edge_in,
    w_edge_out,
    w_node_in,
    w_node_out,
    w_coarse_in,
    w_coarse_out,
    d_fine,
    d_coarse,
):
    owned = nodes.shape[0]
    slots = ghost_rows.shape[2]
    coarse = d_coarse.shape[0]
    n_gx, n_gy = lax.axis_size(GX), lax.axis_size("gy")
    place = jnp.stack([lax.axis_index(GX), lax.axis_index("gy"), n_gx, n_gy]).astype(jnp.int32)

    out_up, out_down, out_mid, gcol = call_pick(place, ghost_count, ghost_rows, nodes)
    up = lax.ppermute(out_up, GX, ring(n_gx, 1))
    down = lax.ppermute(out_down, GX, ring(n_gx, -1))
    recvs, rcol = call_own(edge_count, edge_recv, nodes)
    up, down, recvs = lax.optimization_barrier((up, down, recvs))

    yup = lax.ppermute(
        jnp.concatenate(
            [up[2 * slots :], out_mid[slots:], down[2 * slots :], d_coarse[coarse - BAND :]]
        ),
        "gy",
        ring(n_gy, 1),
    )
    ydown = lax.ppermute(
        jnp.concatenate([up[:slots], out_mid[:slots], down[:slots], d_coarse[:BAND]]),
        "gy",
        ring(n_gy, -1),
    )
    sown, scol = call_own(edge_count, edge_send, nodes)

    (senders, act, slope, fine_out, summed, nact, nslope, window, wlow, whigh) = call_forward(
        edge_count,
        edge_recv,
        coarse + 2 * BAND,
        scol,
        rcol,
        sown,
        recvs,
        up,
        down,
        yup,
        ydown,
        nodes,
        pool_map,
        w_edge_in,
        w_edge_out,
        w_node_in,
        w_node_out,
    )

    nlow = lax.ppermute(whigh, "gy", ring(n_gy, 1))
    nhigh = lax.ppermute(wlow, "gy", ring(n_gy, -1))

    coarse_out, d_node, d_edge, grads = call_backward(
        (rcol, senders, recvs, act, slope),
        (
            window,
            nlow,
            nhigh,
            yup[3 * slots :],
            ydown[3 * slots :],
            d_coarse,
            d_fine,
            pool_map,
            nodes,
            summed,
            nact,
            nslope,
            w_edge_in,
            w_edge_out,
            w_node_in,
            w_node_out,
            w_coarse_in,
            w_coarse_out,
        ),
    )
    own = scattered(grads)
    r_down, r_up, r_own = call_ghost(edge_count, edge_send, d_edge, w_edge_in, owned, slots)
    own, r_down, r_up, r_own = lax.optimization_barrier((own, r_down, r_up, r_own))
    high = lax.ppermute(r_down, "gy", ring(n_gy, -1))
    low = lax.ppermute(r_up, "gy", ring(n_gy, 1))
    own = to_all(own, "gy").astype(f32).sum(axis=0).astype(bf16)
    d_own = call_local(edge_count, edge_send, edge_recv, d_edge, d_node, w_edge_in)
    ret_up = lax.ppermute(
        jnp.concatenate([low[:slots], r_own[slots:], high[:slots]]), GX, ring(n_gx, -1)
    )
    ret_down = lax.ppermute(
        jnp.concatenate([low[2 * slots :], r_own[:slots], high[2 * slots :]]), GX, ring(n_gx, 1)
    )
    own, ret_down, ret_up, d_own = lax.optimization_barrier((own, ret_down, ret_up, d_own))
    sums = to_all(own, GX).reshape(grads.shape)
    grad_nodes = call_return(
        place, ghost_count, ghost_rows, gcol, ret_down, ret_up, low, high, d_own
    )
    scaled = call_scale(1.0 / (owned * n_gx * n_gy) ** 0.5, sums)
    return (fine_out, coarse_out, grad_nodes, *scaled)


def solution(mesh):
    torus = Mesh(mesh.devices.reshape(4, 4, 2, mesh.shape["gy"]), GX_GY)
    in_specs = (
        P(GX_GY, None),
        P(GX_GY, None, None),
        P(GX_GY, None),
        P(GX_GY, None),
        P(GX_GY, None),
        P(GX_GY),
        P(GX_GY, None),
        P(),
        P(),
        P(),
        P(),
        P(),
        P(),
        P(GX_GY, None),
        P(GX_GY, None),
    )
    out_specs = (P(GX_GY, None), P(GX_GY, None), P(GX_GY, None), P(), P(), P(), P(), P(), P())
    return jax.shard_map(body, mesh=torus, in_specs=in_specs, out_specs=out_specs, check_vma=False)
```

```python
import jax
import jax.numpy as jnp
from jax import lax
from jax.experimental import pallas as pl
from jax.experimental.pallas import tpu as pltpu
from jax.sharding import Mesh
from jax.sharding import PartitionSpec as P

BAND = 32
LAT = 128
LOW = 512
BITS = 9
CHUNK = 1024
FWD_CHUNK = 512
FWD_MIB = BWD_MIB = 20
GX_GY = ("gx_0", "gx_1", "gx_2", "gy")
GX = ("gx_0", "gx_1", "gx_2")
CHIPS = ("gx_0", "gx_1")
CORE = "gx_2"
ACROSS = (-1, -1, -1, 0, 0, 1, 1, 1)
ALONG = (-1, 0, 1, -1, 1, -1, 0, 1)
MIB = 1024 * 1024

f32 = jnp.float32
bf16 = jnp.bfloat16


def mm(left, right):
    return jnp.dot(left, right, preferred_element_type=f32)


def mm_nt(left, right):
    return lax.dot_general(left, right, (((1,), (1,)), ((), ())), preferred_element_type=f32)


def mm_tn(left, right):
    return lax.dot_general(left, right, (((0,), (0,)), ((), ())), preferred_element_type=f32)


def wide(table):
    groups = table.shape[0] // LOW
    return jnp.concatenate([table[i * LOW : (i + 1) * LOW] for i in range(groups)], axis=1)


def tall(table):
    groups = table.shape[1] // LAT
    return jnp.concatenate([table[:, i * LAT : (i + 1) * LAT] for i in range(groups)], axis=0)


def in_columns(row):
    parts = []
    for j in range(row.shape[1] // LAT):
        parts.append(jnp.broadcast_to(row[:, j * LAT : (j + 1) * LAT], (LAT, LAT)).T)
    return jnp.concatenate(parts, axis=0).astype(jnp.int16)


def one_hot(col, rows):
    lanes = lax.broadcasted_iota(jnp.int16, col.shape, 1)
    one, zero = jnp.ones((), bf16), jnp.zeros((), bf16)
    return jnp.concatenate(
        [jnp.where(col == lanes + j * LAT, one, zero) for j in range(rows // LAT)], axis=1
    )


def one_hot_t(row, rows):
    ids = lax.broadcasted_iota(jnp.int16, (rows, row.shape[1]), 0)
    col = jnp.broadcast_to(row, (16, row.shape[1])).astype(jnp.int16)
    col = jnp.concatenate([col] * (rows // 16), axis=0)
    return jnp.where(ids == col, jnp.ones((), bf16), jnp.zeros((), bf16))


def take(col, table):
    got = mm(one_hot(col & (LOW - 1), LOW), table)
    group = col.astype(jnp.int32) >> BITS
    total = jnp.zeros((col.shape[0], LAT), f32)
    for i in range(table.shape[1] // LAT):
        total = jnp.where(group == i, got[:, i * LAT : (i + 1) * LAT], total)
    return total.astype(bf16)


def put(row, col, values, groups):
    group = col >> BITS
    zero = jnp.zeros((), bf16)
    spread = jnp.concatenate([jnp.where(group == i, values, zero) for i in range(groups)], axis=1)
    return mm(one_hot_t(row & (LOW - 1), LOW), spread)


def sigmoid(v):
    return 0.5 + 0.5 * jnp.tanh(0.5 * v)


def act_and_slope(v):
    s = sigmoid(v)
    return v * s, s * (1.0 + v * (1.0 - s))


def live_row(row, first, count):
    ids = lax.broadcasted_iota(jnp.int32, row.shape, 1) + first
    return jnp.where(ids < count, row, -1)


def live_slots(place_ref, count_ref, k):
    a = place_ref[0] + ACROSS[k]
    b = place_ref[1] + ALONG[k]
    inside = (a >= 0) & (a < place_ref[2]) & (b >= 0) & (b < place_ref[3])
    return jnp.where(inside, count_ref[0, k], 0)


def pick_kernel(place_ref, count_ref, rows_hbm, nodes_hbm, up_ref, down_ref, mid_ref, cols_ref, rows, nodes, sems):
    copies = (
        pltpu.make_async_copy(nodes_hbm, nodes, sems.at[0]),
        pltpu.make_async_copy(rows_hbm, rows, sems.at[1]),
    )
    for copy in copies:
        copy.start()
    for copy in copies:
        copy.wait()
    table = wide(nodes[...])
    slots = rows.shape[2]
    for k in range(8):
        row = live_row(rows[0, k : k + 1, :], 0, live_slots(place_ref, count_ref, k))
        col = in_columns(row)
        cols_ref[k * slots : (k + 1) * slots, :] = col
        got = take(col, table)
        if k < 3:
            down_ref[k * slots : (k + 1) * slots, :] = got
        elif k < 5:
            mid_ref[(k - 3) * slots : (k - 2) * slots, :] = got
        else:
            up_ref[(k - 5) * slots : (k - 4) * slots, :] = got


def own_kernel(count_ref, index_ref, nodes_ref, out_ref, cols_ref):
    table = wide(nodes_ref[...])
    col = in_columns(live_row(index_ref[...], 0, count_ref[0]))
    cols_ref[...] = col
    out_ref[...] = take(col, table)


def forward_kernel(
    count_ref,
    recv_ref,
    scol_ref,
    rcol_ref,
    sown_ref,
    recvs_ref,
    up_ref,
    down_ref,
    yup_ref,
    ydown_ref,
    nodes_ref,
    pool_ref,
    wei_ref,
    weo_ref,
    wni_ref,
    wno_ref,
    senders_ref,
    act_ref,
    slope_ref,
    fine_ref,
    summed_ref,
    nact_ref,
    nslope_ref,
    window_ref,
    wlow_ref,
    whigh_ref,
    table,
):
    slots = up_ref.shape[0] // 3

    def block(ref, i):
        return ref[i * slots : (i + 1) * slots, :]

    blocks = (
        block(ydown_ref, 2),
        block(down_ref, 1),
        block(yup_ref, 2),
        block(ydown_ref, 1),
        block(yup_ref, 1),
        block(ydown_ref, 0),
        block(up_ref, 1),
        block(yup_ref, 0),
    )
    for k in range(8):
        table[(k % 2) * slots : (k % 2 + 1) * slots, (k // 2) * LAT : (k // 2 + 1) * LAT] = blocks[k]

    owned = nodes_ref.shape[0]
    edges = recv_ref.shape[1]
    chunks = [slice(first, first + FWD_CHUNK) for first in range(0, edges, FWD_CHUNK)]
    recv = live_row(recv_ref[...], 0, count_ref[0])

    def senders_of(here):
        senders = take(scol_ref[here, :] - owned, table[...]) + sown_ref[here, :]
        senders_ref[here, :] = senders
        return senders

    def messages_of(here, senders):
        pre = mm(jnp.concatenate([senders, recvs_ref[here, :]], axis=1), wei_ref[...])
        act, slope = act_and_slope(pre)
        act = act.astype(bf16)
        act_ref[here, :] = act
        slope_ref[here, :] = slope.astype(bf16)
        return mm(act, weo_ref[...]).astype(bf16)

    def summed_of(here, message):
        return put(recv[:, here], rcol_ref[here, :], message, owned // LOW)

    total = jnp.zeros((LOW, owned // LOW * LAT), f32)
    ahead = senders_of(chunks[0])
    behind = None
    for i, here in enumerate(chunks):
        senders = ahead
        if i + 1 < len(chunks):
            ahead = senders_of(chunks[i + 1])
        message = messages_of(here, senders)
        if behind is not None:
            total = total + summed_of(*behind)
        behind = (here, message)
    summed = tall(total + summed_of(*behind)).astype(bf16)
    summed_ref[...] = summed
    nodes = nodes_ref[...]
    pre = mm(jnp.concatenate([nodes, summed], axis=1), wni_ref[...])
    act, slope = act_and_slope(pre)
    act = act.astype(bf16)
    nact_ref[...] = act
    nslope_ref[...] = slope.astype(bf16)
    fine = (nodes.astype(f32) + mm(act, wno_ref[...])).astype(bf16)
    fine_ref[...] = fine
    rows = window_ref.shape[0]
    window = mm(one_hot_t(pool_ref[...], rows), fine)
    window_ref[...] = window
    wlow_ref[...] = window[: 2 * BAND].astype(bf16)
    whigh_ref[...] = window[rows - 2 * BAND :].astype(bf16)


def backward_kernel(
    place_ref,
    rcol_ref,
    senders_ref,
    recvs_ref,
    act_ref,
    slope_ref,
    window_ref,
    nlow_ref,
    nhigh_ref,
    dcl_ref,
    dch_ref,
    dcoarse_ref,
    dfine_ref,
    pool_ref,
    nodes_ref,
    summed_ref,
    nact_ref,
    nslope_ref,
    wei_ref,
    weo_ref,
    wni_ref,
    wno_ref,
    wci_ref,
    wco_ref,
    coarse_ref,
    dnode_ref,
    dedge_ref,
    keep_ref,
    give_ref,
    table,
    grads_ref,
):
    window = window_ref[...]
    rows = window.shape[0]
    total = jnp.concatenate(
        [
            window[: 2 * BAND] + nlow_ref[...].astype(f32),
            window[2 * BAND : rows - 2 * BAND],
            window[rows - 2 * BAND :] + nhigh_ref[...].astype(f32),
        ],
        axis=0,
    )
    coarse_in = (0.125 * total).astype(bf16)
    d_coarse = jnp.concatenate([dcl_ref[...], dcoarse_ref[...], dch_ref[...]], axis=0)
    act, slope = act_and_slope(mm(coarse_in, wci_ref[...]))
    act = act.astype(bf16)
    coarse_out = (coarse_in.astype(f32) + mm(act, wco_ref[...])).astype(bf16)
    coarse_ref[...] = coarse_out[BAND : rows - BAND]
    d_pre = (mm_nt(d_coarse, wco_ref[...]) * slope).astype(bf16)
    d_in = (d_coarse.astype(f32) + mm_nt(d_pre, wci_ref[...])).astype(bf16)
    inner = slice(BAND, rows - BAND)
    g_ci = mm_tn(coarse_in[inner], d_pre[inner])
    g_co = mm_tn(act[inner], d_coarse[inner])
    reach = jnp.concatenate([d_in, jnp.zeros((2 * LAT - rows, LAT), bf16)], axis=0)
    parent = mm(one_hot(in_columns(pool_ref[...]), 2 * LAT), reach)
    d_total = dfine_ref[...].astype(f32) + 0.125 * parent
    d_out = d_total.astype(bf16)
    d_node = (mm_nt(d_out, wno_ref[...]) * nslope_ref[...].astype(f32)).astype(bf16)
    back = mm_nt(d_node, wni_ref[...])
    dnode_ref[...] = d_total + back[:, :LAT]
    table[...] = wide(back[:, LAT:].astype(bf16))
    g_ni = mm_tn(jnp.concatenate([nodes_ref[...], summed_ref[...]], axis=1), d_node)
    g_no = mm_tn(nact_ref[...], d_out)
    grads_ref[4 * LAT : 6 * LAT, :] = g_ni.astype(bf16)
    grads_ref[3 * LAT : 4 * LAT, :] = g_no.astype(bf16)
    grads_ref[6 * LAT : 7 * LAT, :] = g_ci.astype(bf16)
    grads_ref[7 * LAT :, :] = g_co.astype(bf16)

    edges = rcol_ref.shape[0]
    g_ei = jnp.zeros((2 * LAT, LAT), f32)
    g_eo = jnp.zeros((LAT, LAT), f32)
    for first in range(0, edges, CHUNK):
        here = slice(first, first + CHUNK)
        d_message = take(rcol_ref[here, :], table[...])
        d_pre = (mm_nt(d_message, weo_ref[...]) * slope_ref[here, :].astype(f32)).astype(bf16)
        dedge_ref[here, :] = d_pre
        ends = jnp.concatenate([senders_ref[here, :], recvs_ref[here, :], act_ref[here, :]], axis=1)
        both = mm_tn(ends, jnp.concatenate([d_pre, d_message], axis=1))
        g_ei = g_ei + both[: 2 * LAT, :LAT]
        g_eo = g_eo + both[2 * LAT :, LAT:]
    grads_ref[: 2 * LAT, :] = g_ei.astype(bf16)
    grads_ref[2 * LAT : 3 * LAT, :] = g_eo.astype(bf16)
    half = keep_ref.shape[0]
    keep = pl.multiple_of(place_ref[4] * half, half)
    keep_ref[...] = grads_ref[pl.ds(keep, half), :]
    give_ref[...] = grads_ref[pl.ds(pl.multiple_of(half - keep, half), half), :]


def ghost_kernel(count_ref, send_ref, dedge_ref, wei_ref, rdown_ref, rup_ref, rown_ref, *, owned):
    send = live_row(send_ref[...], 0, count_ref[0]) - owned
    total = put(send, in_columns(send), dedge_ref[...], 4)
    ghosts = mm_nt(tall(total).astype(bf16), wei_ref[:LAT, :]).astype(bf16)
    slots = ghosts.shape[0] // 8
    for place, (ref, i) in enumerate(
        (
            (rup_ref, 2),
            (rown_ref, 0),
            (rdown_ref, 2),
            (rup_ref, 1),
            (rdown_ref, 1),
            (rup_ref, 0),
            (rown_ref, 1),
            (rdown_ref, 0),
        )
    ):
        ref[i * slots : (i + 1) * slots, :] = ghosts[place * slots : (place + 1) * slots]


def local_kernel(count_ref, send_ref, recv_ref, dedge_ref, dnode_ref, wei_ref, out_ref):
    groups = out_ref.shape[0] // LOW
    d_pre = dedge_ref[...]
    send = live_row(send_ref[...], 0, count_ref[0])
    recv = live_row(recv_ref[...], 0, count_ref[0])
    by_send = tall(put(send, in_columns(send), d_pre, groups)).astype(bf16)
    by_recv = tall(put(recv, in_columns(recv), d_pre, groups)).astype(bf16)
    out_ref[...] = dnode_ref[...] + mm_nt(
        jnp.concatenate([by_send, by_recv], axis=1),
        jnp.concatenate([wei_ref[:LAT, :], wei_ref[LAT:, :]], axis=1),
    )


def return_kernel(
    place_ref,
    count_ref,
    rows_ref,
    cols_ref,
    down_ref,
    up_ref,
    mid_low_ref,
    mid_high_ref,
    part_ref,
    out_ref,
):
    slots = rows_ref.shape[2]
    groups = out_ref.shape[0] // LOW
    total = jnp.zeros((LOW, groups * LAT), f32)
    for k in range(8):
        row = live_row(rows_ref[0, k : k + 1, :], 0, live_slots(place_ref, count_ref, k))
        col = cols_ref[k * slots : (k + 1) * slots, :]
        if k < 3:
            got = down_ref[k * slots : (k + 1) * slots, :]
        elif k == 3:
            got = mid_low_ref[slots : 2 * slots, :]
        elif k == 4:
            got = mid_high_ref[slots : 2 * slots, :]
        else:
            got = up_ref[(k - 5) * slots : (k - 4) * slots, :]
        total = total + put(row, col, got, groups)
    out_ref[...] = part_ref[...] + tall(total)


def scale_kernel(scale, place_ref, kept_ref, other_ref, *grad_refs):
    def write(halves):
        half = kept_ref.shape[0]
        for ref, first in zip(grad_refs, (0, 2 * LAT, 4 * LAT, 3 * LAT, 6 * LAT, 7 * LAT)):
            rows = ref.shape[0]
            source = halves[first // half]
            start = first % half
            ref[...] = source[start : start + rows, :].astype(f32) * scale

    @pl.when(place_ref[4] == 0)
    def _():
        write((kept_ref, other_ref))

    @pl.when(place_ref[4] != 0)
    def _():
        write((other_ref, kept_ref))


def scalars():
    return pl.BlockSpec(memory_space=pltpu.SMEM)


def inside(count):
    return [pl.BlockSpec(memory_space=pltpu.VMEM)] * count


def hbm():
    return pl.BlockSpec(memory_space=pltpu.HBM)


def shape(dims, dtype):
    return jax.ShapeDtypeStruct(dims, dtype)


def params(mib):
    return pltpu.CompilerParams(vmem_limit_bytes=mib * MIB)


def cost(flops, moved):
    return pl.CostEstimate(flops=flops, bytes_accessed=moved, transcendentals=0)


def scattered(grads):
    got = lax.all_to_all(grads.reshape(lax.axis_size(CHIPS), -1, LAT), CHIPS, 0, 0, tiled=True)
    return got.astype(f32).sum(axis=0).astype(bf16)


def to_all(own, axis):
    pieces = jnp.broadcast_to(own[None], (lax.axis_size(axis), *own.shape))
    return lax.all_to_all(pieces, axis, 0, 0, tiled=True)


def call_pick(place, ghost_count, ghost_rows, nodes):
    slots = ghost_rows.shape[2]
    return pl.pallas_call(
        pick_kernel,
        out_shape=(
            shape((3 * slots, LAT), bf16),
            shape((3 * slots, LAT), bf16),
            shape((2 * slots, LAT), bf16),
            shape((8 * slots, LAT), jnp.int16),
        ),
        in_specs=[scalars(), scalars(), hbm(), hbm()],
        out_specs=tuple(inside(4)),
        scratch_shapes=[
            pltpu.VMEM(ghost_rows.shape, jnp.int32),
            pltpu.VMEM(nodes.shape, bf16),
            pltpu.SemaphoreType.DMA((2,)),
        ],
        compiler_params=params(32),
        cost_estimate=cost(2 * 2048 * 512 * 256, MIB),
        name="pick",
    )(place, ghost_count, ghost_rows, nodes)


def call_own(edge_count, index, nodes):
    edges = index.shape[1]
    return pl.pallas_call(
        own_kernel,
        out_shape=(shape((edges, LAT), bf16), shape((edges, LAT), jnp.int16)),
        in_specs=[scalars(), *inside(2)],
        out_specs=tuple(inside(2)),
        compiler_params=params(16),
        cost_estimate=cost(2 * 4096 * 512 * 256, 2 * MIB),
        name="own_rows",
    )(edge_count, index, nodes)


def call_forward(edge_count, recv, rows, *plain):
    edges, owned = recv.shape[1], plain[8].shape[0]
    edge16 = shape((edges, LAT), bf16)
    node16 = shape((owned, LAT), bf16)
    band = shape((2 * BAND, LAT), bf16)
    outs = (edge16,) * 3 + (node16,) * 4 + (shape((rows, LAT), f32), band, band)
    return pl.pallas_call(
        forward_kernel,
        out_shape=outs,
        in_specs=[scalars(), *inside(1 + len(plain))],
        out_specs=tuple(inside(len(outs))),
        scratch_shapes=[pltpu.VMEM((LOW, 4 * LAT), bf16)],
        compiler_params=params(FWD_MIB),
        cost_estimate=cost(2 * 4096 * 512 * 1024, 8 * MIB),
        name="forward",
    )(edge_count, recv, *plain)


def call_backward(place, edge_arrays, plain):
    edges = edge_arrays[0].shape[0]
    owned, coarse = plain[8].shape[0], plain[5].shape[0]
    return pl.pallas_call(
        backward_kernel,
        out_shape=(
            shape((coarse, LAT), bf16),
            shape((owned, LAT), f32),
            shape((edges, LAT), bf16),
            shape((4 * LAT, LAT), bf16),
            shape((4 * LAT, LAT), bf16),
        ),
        in_specs=[scalars(), *inside(len(edge_arrays) + len(plain))],
        out_specs=tuple(inside(5)),
        scratch_shapes=[
            pltpu.VMEM((LOW, owned // LOW * LAT), bf16),
            pltpu.VMEM((8 * LAT, LAT), bf16),
        ],
        compiler_params=params(BWD_MIB),
        cost_estimate=cost(2 * 4096 * 512 * 512, 8 * MIB),
        name="backward",
    )(place, *edge_arrays, *plain)


def call_ghost(edge_count, send, d_edge, w_edge_in, owned, slots):
    return pl.pallas_call(
        lambda *refs: ghost_kernel(*refs, owned=owned),
        out_shape=(
            shape((3 * slots, LAT), bf16),
            shape((3 * slots, LAT), bf16),
            shape((2 * slots, LAT), bf16),
        ),
        in_specs=[scalars(), *inside(3)],
        out_specs=tuple(inside(3)),
        compiler_params=params(16),
        cost_estimate=cost(2 * 4096 * 512 * 512, 3 * MIB),
        name="ghost_grads",
    )(edge_count, send, d_edge, w_edge_in)


def call_local(edge_count, send, recv, d_edge, d_node, w_edge_in):
    return pl.pallas_call(
        local_kernel,
        out_shape=shape(d_node.shape, f32),
        in_specs=[scalars(), *inside(5)],
        out_specs=inside(1)[0],
        compiler_params=params(16),
        cost_estimate=cost(2 * 2 * 4096 * 512 * 256, 3 * MIB),
        name="local",
    )(edge_count, send, recv, d_edge, d_node, w_edge_in)


def call_return(place, ghost_count, *arrays):
    owned = arrays[-1].shape[0]
    return pl.pallas_call(
        return_kernel,
        out_shape=shape((owned, LAT), f32),
        in_specs=[scalars(), scalars(), *inside(len(arrays))],
        out_specs=inside(1)[0],
        compiler_params=params(16),
        cost_estimate=cost(2 * 2048 * 512 * 256, 2 * MIB),
        name="returned",
    )(place, ghost_count, *arrays)


def call_scale(scale, place, kept, other):
    heights = (2 * LAT, LAT, 2 * LAT, LAT, LAT, LAT)
    return pl.pallas_call(
        lambda *refs: scale_kernel(scale, *refs),
        out_shape=tuple(shape((h, LAT), f32) for h in heights),
        in_specs=[scalars(), *inside(2)],
        out_specs=tuple(inside(6)),
        compiler_params=params(8),
        name="scaled",
    )(place, kept, other)


def ring(n, shift):
    return [(i, (i + shift) % n) for i in range(n)]


def body(
    nodes,
    ghost_rows,
    ghost_count,
    edge_send,
    edge_recv,
    edge_count,
    pool_map,
    w_edge_in,
    w_edge_out,
    w_node_in,
    w_node_out,
    w_coarse_in,
    w_coarse_out,
    d_fine,
    d_coarse,
):
    owned = nodes.shape[0]
    slots = ghost_rows.shape[2]
    coarse = d_coarse.shape[0]
    n_gx, n_gy = lax.axis_size(GX), lax.axis_size("gy")
    place = jnp.stack(
        [lax.axis_index(GX), lax.axis_index("gy"), n_gx, n_gy, lax.axis_index(CORE)]
    ).astype(jnp.int32)

    out_up, out_down, out_mid, gcol = call_pick(place, ghost_count, ghost_rows, nodes)
    up = lax.ppermute(out_up, GX, ring(n_gx, 1))
    down = lax.ppermute(out_down, GX, ring(n_gx, -1))
    recvs, rcol = call_own(edge_count, edge_recv, nodes)
    up, down, recvs = lax.optimization_barrier((up, down, recvs))

    yup = lax.ppermute(
        jnp.concatenate(
            [up[2 * slots :], out_mid[slots:], down[2 * slots :], d_coarse[coarse - BAND :]]
        ),
        "gy",
        ring(n_gy, 1),
    )
    ydown = lax.ppermute(
        jnp.concatenate([up[:slots], out_mid[:slots], down[:slots], d_coarse[:BAND]]),
        "gy",
        ring(n_gy, -1),
    )
    sown, scol = call_own(edge_count, edge_send, nodes)

    (senders, act, slope, fine_out, summed, nact, nslope, window, wlow, whigh) = call_forward(
        edge_count,
        edge_recv,
        coarse + 2 * BAND,
        scol,
        rcol,
        sown,
        recvs,
        up,
        down,
        yup,
        ydown,
        nodes,
        pool_map,
        w_edge_in,
        w_edge_out,
        w_node_in,
        w_node_out,
    )

    nlow = lax.ppermute(whigh, "gy", ring(n_gy, 1))
    nhigh = lax.ppermute(wlow, "gy", ring(n_gy, -1))

    coarse_out, d_node, d_edge, keep, give = call_backward(
        place,
        (rcol, senders, recvs, act, slope),
        (
            window,
            nlow,
            nhigh,
            yup[3 * slots :],
            ydown[3 * slots :],
            d_coarse,
            d_fine,
            pool_map,
            nodes,
            summed,
            nact,
            nslope,
            w_edge_in,
            w_edge_out,
            w_node_in,
            w_node_out,
            w_coarse_in,
            w_coarse_out,
        ),
    )
    swap = ring(lax.axis_size(CORE), 1)
    got = lax.ppermute(give, CORE, swap)
    own = scattered((keep.astype(f32) + got.astype(f32)).astype(bf16))
    r_down, r_up, r_own = call_ghost(edge_count, edge_send, d_edge, w_edge_in, owned, slots)
    own, r_down, r_up, r_own = lax.optimization_barrier((own, r_down, r_up, r_own))
    high = lax.ppermute(r_down, "gy", ring(n_gy, -1))
    low = lax.ppermute(r_up, "gy", ring(n_gy, 1))
    own = to_all(own, "gy").astype(f32).sum(axis=0).astype(bf16)
    d_own = call_local(edge_count, edge_send, edge_recv, d_edge, d_node, w_edge_in)
    ret_up = lax.ppermute(
        jnp.concatenate([low[:slots], r_own[slots:], high[:slots]]), GX, ring(n_gx, -1)
    )
    ret_down = lax.ppermute(
        jnp.concatenate([low[2 * slots :], r_own[:slots], high[2 * slots :]]), GX, ring(n_gx, 1)
    )
    own, ret_down, ret_up, d_own = lax.optimization_barrier((own, ret_down, ret_up, d_own))
    half = to_all(own, CHIPS).reshape(keep.shape)
    other = lax.ppermute(half, CORE, swap)
    grad_nodes = call_return(
        place, ghost_count, ghost_rows, gcol, ret_down, ret_up, low, high, d_own
    )
    scaled = call_scale(1.0 / (owned * n_gx * n_gy) ** 0.5, place, half, other)
    return (fine_out, coarse_out, grad_nodes, *scaled)


def solution(mesh):
    torus = Mesh(mesh.devices.reshape(4, 4, 2, mesh.shape["gy"]), GX_GY)
    in_specs = (
        P(GX_GY, None),
        P(GX_GY, None, None),
        P(GX_GY, None),
        P(GX_GY, None),
        P(GX_GY, None),
        P(GX_GY),
        P(GX_GY, None),
        P(),
        P(),
        P(),
        P(),
        P(),
        P(),
        P(GX_GY, None),
        P(GX_GY, None),
    )
    out_specs = (P(GX_GY, None), P(GX_GY, None), P(GX_GY, None), P(), P(), P(), P(), P(), P())
    return jax.shard_map(body, mesh=torus, in_specs=in_specs, out_specs=out_specs, check_vma=False)
```

```python
import jax
import jax.numpy as jnp
from jax import lax
from jax.experimental import pallas as pl
from jax.experimental.pallas import tpu as pltpu
from jax.sharding import Mesh
from jax.sharding import PartitionSpec as P

BAND = 32
LAT = 128
LOW = 512
BITS = 9
CHUNK = 1024
FWD_CHUNK = 512
FWD_MIB = BWD_MIB = 20
GX_GY = ("gx_0", "gx_1", "gx_2", "gy")
GX = ("gx_0", "gx_1", "gx_2")
CHIPS = ("gx_0", "gx_1")
CORE = "gx_2"
ACROSS = (-1, -1, -1, 0, 0, 1, 1, 1)
ALONG = (-1, 0, 1, -1, 1, -1, 0, 1)
MIB = 1024 * 1024

f32 = jnp.float32
bf16 = jnp.bfloat16


def mm(left, right):
    return jnp.dot(left, right, preferred_element_type=f32)


def mm_nt(left, right):
    return lax.dot_general(left, right, (((1,), (1,)), ((), ())), preferred_element_type=f32)


def mm_tn(left, right):
    return lax.dot_general(left, right, (((0,), (0,)), ((), ())), preferred_element_type=f32)


def wide(table):
    groups = table.shape[0] // LOW
    return jnp.concatenate([table[i * LOW : (i + 1) * LOW] for i in range(groups)], axis=1)


def tall(table):
    groups = table.shape[1] // LAT
    return jnp.concatenate([table[:, i * LAT : (i + 1) * LAT] for i in range(groups)], axis=0)


def in_columns(row):
    parts = []
    for j in range(row.shape[1] // LAT):
        parts.append(jnp.broadcast_to(row[:, j * LAT : (j + 1) * LAT], (LAT, LAT)).T)
    return jnp.concatenate(parts, axis=0).astype(jnp.int16)


def one_hot(col, rows):
    lanes = lax.broadcasted_iota(jnp.int16, col.shape, 1)
    one, zero = jnp.ones((), bf16), jnp.zeros((), bf16)
    return jnp.concatenate(
        [jnp.where(col == lanes + j * LAT, one, zero) for j in range(rows // LAT)], axis=1
    )


def one_hot_t(row, rows):
    ids = lax.broadcasted_iota(jnp.int16, (rows, row.shape[1]), 0)
    col = jnp.broadcast_to(row, (16, row.shape[1])).astype(jnp.int16)
    col = jnp.concatenate([col] * (rows // 16), axis=0)
    return jnp.where(ids == col, jnp.ones((), bf16), jnp.zeros((), bf16))


def take(col, table):
    got = mm(one_hot(col & (LOW - 1), LOW), table)
    group = col.astype(jnp.int32) >> BITS
    total = jnp.zeros((col.shape[0], LAT), f32)
    for i in range(table.shape[1] // LAT):
        total = jnp.where(group == i, got[:, i * LAT : (i + 1) * LAT], total)
    return total.astype(bf16)


def put(row, col, values, groups):
    group = col >> BITS
    zero = jnp.zeros((), bf16)
    spread = jnp.concatenate([jnp.where(group == i, values, zero) for i in range(groups)], axis=1)
    return mm(one_hot_t(row & (LOW - 1), LOW), spread)


def sigmoid(v):
    return 0.5 + 0.5 * jnp.tanh(0.5 * v)


def act_and_slope(v):
    s = sigmoid(v)
    return v * s, s * (1.0 + v * (1.0 - s))


def live_row(row, first, count):
    ids = lax.broadcasted_iota(jnp.int32, row.shape, 1) + first
    return jnp.where(ids < count, row, -1)


def live_slots(place_ref, count_ref, k):
    a = place_ref[0] + ACROSS[k]
    b = place_ref[1] + ALONG[k]
    inside = (a >= 0) & (a < place_ref[2]) & (b >= 0) & (b < place_ref[3])
    return jnp.where(inside, count_ref[0, k], 0)


def pick_kernel(place_ref, count_ref, rows_hbm, nodes_hbm, up_ref, down_ref, mid_ref, cols_ref, rows, nodes, sems):
    copies = (
        pltpu.make_async_copy(nodes_hbm, nodes, sems.at[0]),
        pltpu.make_async_copy(rows_hbm, rows, sems.at[1]),
    )
    for copy in copies:
        copy.start()
    for copy in copies:
        copy.wait()
    table = wide(nodes[...])
    slots = rows.shape[2]
    for k in range(8):
        row = live_row(rows[0, k : k + 1, :], 0, live_slots(place_ref, count_ref, k))
        col = in_columns(row)
        cols_ref[k * slots : (k + 1) * slots, :] = col
        got = take(col, table)
        if k < 3:
            down_ref[k * slots : (k + 1) * slots, :] = got
        elif k < 5:
            mid_ref[(k - 3) * slots : (k - 2) * slots, :] = got
        else:
            up_ref[(k - 5) * slots : (k - 4) * slots, :] = got


def own_kernel(count_ref, index_ref, nodes_ref, out_ref, cols_ref):
    table = wide(nodes_ref[...])
    col = in_columns(live_row(index_ref[...], 0, count_ref[0]))
    cols_ref[...] = col
    out_ref[...] = take(col, table)


def forward_kernel(
    count_ref,
    recv_ref,
    scol_ref,
    rcol_ref,
    sown_ref,
    recvs_ref,
    up_ref,
    down_ref,
    yup_ref,
    ydown_ref,
    nodes_ref,
    pool_ref,
    wei_ref,
    weo_ref,
    wni_ref,
    wno_ref,
    senders_ref,
    act_ref,
    slope_ref,
    fine_ref,
    summed_ref,
    nact_ref,
    nslope_ref,
    window_ref,
    wlow_ref,
    whigh_ref,
    table,
):
    slots = up_ref.shape[0] // 3

    def block(ref, i):
        return ref[i * slots : (i + 1) * slots, :]

    blocks = (
        block(ydown_ref, 2),
        block(down_ref, 1),
        block(yup_ref, 2),
        block(ydown_ref, 1),
        block(yup_ref, 1),
        block(ydown_ref, 0),
        block(up_ref, 1),
        block(yup_ref, 0),
    )
    for k in range(8):
        table[(k % 2) * slots : (k % 2 + 1) * slots, (k // 2) * LAT : (k // 2 + 1) * LAT] = blocks[k]

    owned = nodes_ref.shape[0]
    edges = recv_ref.shape[1]
    chunks = [slice(first, first + FWD_CHUNK) for first in range(0, edges, FWD_CHUNK)]
    recv = live_row(recv_ref[...], 0, count_ref[0])

    def senders_of(here):
        senders = take(scol_ref[here, :] - owned, table[...]) + sown_ref[here, :]
        senders_ref[here, :] = senders
        return senders

    def messages_of(here, senders):
        pre = mm(jnp.concatenate([senders, recvs_ref[here, :]], axis=1), wei_ref[...])
        act, slope = act_and_slope(pre)
        act = act.astype(bf16)
        act_ref[here, :] = act
        slope_ref[here, :] = slope.astype(bf16)
        return mm(act, weo_ref[...]).astype(bf16)

    def summed_of(here, message):
        return put(recv[:, here], rcol_ref[here, :], message, owned // LOW)

    total = jnp.zeros((LOW, owned // LOW * LAT), f32)
    ahead = senders_of(chunks[0])
    behind = None
    for i, here in enumerate(chunks):
        senders = ahead
        if i + 1 < len(chunks):
            ahead = senders_of(chunks[i + 1])
        message = messages_of(here, senders)
        if behind is not None:
            total = total + summed_of(*behind)
        behind = (here, message)
    summed = tall(total + summed_of(*behind)).astype(bf16)
    summed_ref[...] = summed
    nodes = nodes_ref[...]
    pre = mm(jnp.concatenate([nodes, summed], axis=1), wni_ref[...])
    act, slope = act_and_slope(pre)
    act = act.astype(bf16)
    nact_ref[...] = act
    nslope_ref[...] = slope.astype(bf16)
    fine = (nodes.astype(f32) + mm(act, wno_ref[...])).astype(bf16)
    fine_ref[...] = fine
    rows = window_ref.shape[0]
    window = mm(one_hot_t(pool_ref[...], rows), fine)
    window_ref[...] = window
    wlow_ref[...] = window[: 2 * BAND].astype(bf16)
    whigh_ref[...] = window[rows - 2 * BAND :].astype(bf16)


def backward_kernel(
    place_ref,
    rcol_ref,
    senders_ref,
    recvs_ref,
    act_ref,
    slope_ref,
    window_ref,
    nlow_ref,
    nhigh_ref,
    dcl_ref,
    dch_ref,
    dcoarse_ref,
    dfine_ref,
    pool_ref,
    nodes_ref,
    summed_ref,
    nact_ref,
    nslope_ref,
    wei_ref,
    weo_ref,
    wni_ref,
    wno_ref,
    wci_ref,
    wco_ref,
    coarse_ref,
    dnode_ref,
    dedge_ref,
    keep_ref,
    give_ref,
    table,
    grads_ref,
):
    window = window_ref[...]
    rows = window.shape[0]
    total = jnp.concatenate(
        [
            window[: 2 * BAND] + nlow_ref[...].astype(f32),
            window[2 * BAND : rows - 2 * BAND],
            window[rows - 2 * BAND :] + nhigh_ref[...].astype(f32),
        ],
        axis=0,
    )
    coarse_in = (0.125 * total).astype(bf16)
    d_coarse = jnp.concatenate([dcl_ref[...], dcoarse_ref[...], dch_ref[...]], axis=0)
    act, slope = act_and_slope(mm(coarse_in, wci_ref[...]))
    act = act.astype(bf16)
    coarse_out = (coarse_in.astype(f32) + mm(act, wco_ref[...])).astype(bf16)
    coarse_ref[...] = coarse_out[BAND : rows - BAND]
    d_pre = (mm_nt(d_coarse, wco_ref[...]) * slope).astype(bf16)
    d_in = (d_coarse.astype(f32) + mm_nt(d_pre, wci_ref[...])).astype(bf16)
    inner = slice(BAND, rows - BAND)
    g_ci = mm_tn(coarse_in[inner], d_pre[inner])
    g_co = mm_tn(act[inner], d_coarse[inner])
    reach = jnp.concatenate([d_in, jnp.zeros((2 * LAT - rows, LAT), bf16)], axis=0)
    parent = mm(one_hot(in_columns(pool_ref[...]), 2 * LAT), reach)
    d_total = dfine_ref[...].astype(f32) + 0.125 * parent
    d_out = d_total.astype(bf16)
    d_node = (mm_nt(d_out, wno_ref[...]) * nslope_ref[...].astype(f32)).astype(bf16)
    back = mm_nt(d_node, wni_ref[...])
    dnode_ref[...] = d_total + back[:, :LAT]
    table[...] = wide(back[:, LAT:].astype(bf16))
    g_ni = mm_tn(jnp.concatenate([nodes_ref[...], summed_ref[...]], axis=1), d_node)
    g_no = mm_tn(nact_ref[...], d_out)
    grads_ref[4 * LAT : 6 * LAT, :] = g_ni.astype(bf16)
    grads_ref[3 * LAT : 4 * LAT, :] = g_no.astype(bf16)
    grads_ref[6 * LAT : 7 * LAT, :] = g_ci.astype(bf16)
    grads_ref[7 * LAT :, :] = g_co.astype(bf16)

    edges = rcol_ref.shape[0]
    g_ei = jnp.zeros((2 * LAT, LAT), f32)
    g_eo = jnp.zeros((LAT, LAT), f32)
    for first in range(0, edges, CHUNK):
        here = slice(first, first + CHUNK)
        d_message = take(rcol_ref[here, :], table[...])
        d_pre = (mm_nt(d_message, weo_ref[...]) * slope_ref[here, :].astype(f32)).astype(bf16)
        dedge_ref[here, :] = d_pre
        ends = jnp.concatenate([senders_ref[here, :], recvs_ref[here, :], act_ref[here, :]], axis=1)
        both = mm_tn(ends, jnp.concatenate([d_pre, d_message], axis=1))
        g_ei = g_ei + both[: 2 * LAT, :LAT]
        g_eo = g_eo + both[2 * LAT :, LAT:]
    grads_ref[: 2 * LAT, :] = g_ei.astype(bf16)
    grads_ref[2 * LAT : 3 * LAT, :] = g_eo.astype(bf16)
    half = keep_ref.shape[0]
    keep = pl.multiple_of(place_ref[4] * half, half)
    keep_ref[...] = grads_ref[pl.ds(keep, half), :]
    give_ref[...] = grads_ref[pl.ds(pl.multiple_of(half - keep, half), half), :]


def ghost_kernel(count_ref, send_ref, dedge_ref, wei_ref, rdown_ref, rup_ref, rown_ref, *, owned):
    send = live_row(send_ref[...], 0, count_ref[0]) - owned
    total = put(send, in_columns(send), dedge_ref[...], 4)
    ghosts = mm_nt(tall(total).astype(bf16), wei_ref[:LAT, :]).astype(bf16)
    slots = ghosts.shape[0] // 8
    for place, (ref, i) in enumerate(
        (
            (rup_ref, 2),
            (rown_ref, 0),
            (rdown_ref, 2),
            (rup_ref, 1),
            (rdown_ref, 1),
            (rup_ref, 0),
            (rown_ref, 1),
            (rdown_ref, 0),
        )
    ):
        ref[i * slots : (i + 1) * slots, :] = ghosts[place * slots : (place + 1) * slots]


def local_kernel(count_ref, send_ref, recv_ref, dedge_ref, dnode_ref, wei_ref, out_ref):
    groups = out_ref.shape[0] // LOW
    d_pre = dedge_ref[...]
    send = live_row(send_ref[...], 0, count_ref[0])
    recv = live_row(recv_ref[...], 0, count_ref[0])
    by_send = tall(put(send, in_columns(send), d_pre, groups)).astype(bf16)
    by_recv = tall(put(recv, in_columns(recv), d_pre, groups)).astype(bf16)
    out_ref[...] = dnode_ref[...] + mm_nt(
        jnp.concatenate([by_send, by_recv], axis=1),
        jnp.concatenate([wei_ref[:LAT, :], wei_ref[LAT:, :]], axis=1),
    )


def return_kernel(
    place_ref,
    count_ref,
    rows_ref,
    cols_ref,
    down_ref,
    up_ref,
    mid_low_ref,
    mid_high_ref,
    part_ref,
    out_ref,
):
    slots = rows_ref.shape[2]
    groups = out_ref.shape[0] // LOW
    total = jnp.zeros((LOW, groups * LAT), f32)
    for k in range(8):
        row = live_row(rows_ref[0, k : k + 1, :], 0, live_slots(place_ref, count_ref, k))
        col = cols_ref[k * slots : (k + 1) * slots, :]
        if k < 3:
            got = down_ref[k * slots : (k + 1) * slots, :]
        elif k == 3:
            got = mid_low_ref[slots : 2 * slots, :]
        elif k == 4:
            got = mid_high_ref[slots : 2 * slots, :]
        else:
            got = up_ref[(k - 5) * slots : (k - 4) * slots, :]
        total = total + put(row, col, got, groups)
    out_ref[...] = part_ref[...] + tall(total)


def scale_kernel(scale, place_ref, kept_ref, other_ref, *grad_refs):
    def write(halves):
        half = kept_ref.shape[0]
        for ref, first in zip(grad_refs, (0, 2 * LAT, 4 * LAT, 3 * LAT, 6 * LAT, 7 * LAT)):
            rows = ref.shape[0]
            source = halves[first // half]
            start = first % half
            ref[...] = source[start : start + rows, :].astype(f32) * scale

    @pl.when(place_ref[4] == 0)
    def _():
        write((kept_ref, other_ref))

    @pl.when(place_ref[4] != 0)
    def _():
        write((other_ref, kept_ref))


def scalars():
    return pl.BlockSpec(memory_space=pltpu.SMEM)


def inside(count):
    return [pl.BlockSpec(memory_space=pltpu.VMEM)] * count


def hbm():
    return pl.BlockSpec(memory_space=pltpu.HBM)


def shape(dims, dtype):
    return jax.ShapeDtypeStruct(dims, dtype)


def params(mib):
    return pltpu.CompilerParams(vmem_limit_bytes=mib * MIB)


def cost(flops, moved):
    return pl.CostEstimate(flops=flops, bytes_accessed=moved, transcendentals=0)


def scattered(grads):
    got = lax.all_to_all(grads.reshape(lax.axis_size(CHIPS), -1, LAT), CHIPS, 0, 0, tiled=True)
    return got.astype(f32).sum(axis=0).astype(bf16)


def to_all(own, axis):
    pieces = jnp.broadcast_to(own[None], (lax.axis_size(axis), *own.shape))
    return lax.all_to_all(pieces, axis, 0, 0, tiled=True)


def call_pick(place, ghost_count, ghost_rows, nodes):
    slots = ghost_rows.shape[2]
    return pl.pallas_call(
        pick_kernel,
        out_shape=(
            shape((3 * slots, LAT), bf16),
            shape((3 * slots, LAT), bf16),
            shape((2 * slots, LAT), bf16),
            shape((8 * slots, LAT), jnp.int16),
        ),
        in_specs=[scalars(), scalars(), hbm(), hbm()],
        out_specs=tuple(inside(4)),
        scratch_shapes=[
            pltpu.VMEM(ghost_rows.shape, jnp.int32),
            pltpu.VMEM(nodes.shape, bf16),
            pltpu.SemaphoreType.DMA((2,)),
        ],
        compiler_params=params(32),
        cost_estimate=cost(2 * 2048 * 512 * 256, MIB),
        name="pick",
    )(place, ghost_count, ghost_rows, nodes)


def call_own(edge_count, index, nodes):
    edges = index.shape[1]
    return pl.pallas_call(
        own_kernel,
        out_shape=(shape((edges, LAT), bf16), shape((edges, LAT), jnp.int16)),
        in_specs=[scalars(), *inside(2)],
        out_specs=tuple(inside(2)),
        compiler_params=params(16),
        cost_estimate=cost(2 * 4096 * 512 * 256, 2 * MIB),
        name="own_rows",
    )(edge_count, index, nodes)


def call_forward(edge_count, recv, rows, *plain):
    edges, owned = recv.shape[1], plain[8].shape[0]
    edge16 = shape((edges, LAT), bf16)
    node16 = shape((owned, LAT), bf16)
    band = shape((2 * BAND, LAT), bf16)
    outs = (edge16,) * 3 + (node16,) * 4 + (shape((rows, LAT), f32), band, band)
    return pl.pallas_call(
        forward_kernel,
        out_shape=outs,
        in_specs=[scalars(), *inside(1 + len(plain))],
        out_specs=tuple(inside(len(outs))),
        scratch_shapes=[pltpu.VMEM((LOW, 4 * LAT), bf16)],
        compiler_params=params(FWD_MIB),
        cost_estimate=cost(2 * 4096 * 512 * 1024, 8 * MIB),
        name="forward",
    )(edge_count, recv, *plain)


def call_backward(place, edge_arrays, plain):
    edges = edge_arrays[0].shape[0]
    owned, coarse = plain[8].shape[0], plain[5].shape[0]
    return pl.pallas_call(
        backward_kernel,
        out_shape=(
            shape((coarse, LAT), bf16),
            shape((owned, LAT), f32),
            shape((edges, LAT), bf16),
            shape((4 * LAT, LAT), bf16),
            shape((4 * LAT, LAT), bf16),
        ),
        in_specs=[scalars(), *inside(len(edge_arrays) + len(plain))],
        out_specs=tuple(inside(5)),
        scratch_shapes=[
            pltpu.VMEM((LOW, owned // LOW * LAT), bf16),
            pltpu.VMEM((8 * LAT, LAT), bf16),
        ],
        compiler_params=params(BWD_MIB),
        cost_estimate=cost(2 * 4096 * 512 * 512, 8 * MIB),
        name="backward",
    )(place, *edge_arrays, *plain)


def call_ghost(edge_count, send, d_edge, w_edge_in, owned, slots):
    return pl.pallas_call(
        lambda *refs: ghost_kernel(*refs, owned=owned),
        out_shape=(
            shape((3 * slots, LAT), bf16),
            shape((3 * slots, LAT), bf16),
            shape((2 * slots, LAT), bf16),
        ),
        in_specs=[scalars(), *inside(3)],
        out_specs=tuple(inside(3)),
        compiler_params=params(16),
        cost_estimate=cost(2 * 4096 * 512 * 512, 3 * MIB),
        name="ghost_grads",
    )(edge_count, send, d_edge, w_edge_in)


def call_local(edge_count, send, recv, d_edge, d_node, w_edge_in):
    return pl.pallas_call(
        local_kernel,
        out_shape=shape(d_node.shape, f32),
        in_specs=[scalars(), *inside(5)],
        out_specs=inside(1)[0],
        compiler_params=params(16),
        cost_estimate=cost(2 * 2 * 4096 * 512 * 256, 3 * MIB),
        name="local",
    )(edge_count, send, recv, d_edge, d_node, w_edge_in)


def call_return(place, ghost_count, *arrays):
    owned = arrays[-1].shape[0]
    return pl.pallas_call(
        return_kernel,
        out_shape=shape((owned, LAT), f32),
        in_specs=[scalars(), scalars(), *inside(len(arrays))],
        out_specs=inside(1)[0],
        compiler_params=params(16),
        cost_estimate=cost(2 * 2048 * 512 * 256, 2 * MIB),
        name="returned",
    )(place, ghost_count, *arrays)


def call_scale(scale, place, kept, other):
    heights = (2 * LAT, LAT, 2 * LAT, LAT, LAT, LAT)
    return pl.pallas_call(
        lambda *refs: scale_kernel(scale, *refs),
        out_shape=tuple(shape((h, LAT), f32) for h in heights),
        in_specs=[scalars(), *inside(2)],
        out_specs=tuple(inside(6)),
        compiler_params=params(8),
        name="scaled",
    )(place, kept, other)


def ring(n, shift):
    return [(i, (i + shift) % n) for i in range(n)]


def body(
    nodes,
    ghost_rows,
    ghost_count,
    edge_send,
    edge_recv,
    edge_count,
    pool_map,
    w_edge_in,
    w_edge_out,
    w_node_in,
    w_node_out,
    w_coarse_in,
    w_coarse_out,
    d_fine,
    d_coarse,
):
    owned = nodes.shape[0]
    slots = ghost_rows.shape[2]
    coarse = d_coarse.shape[0]
    n_gx, n_gy = lax.axis_size(GX), lax.axis_size("gy")
    place = jnp.stack(
        [lax.axis_index(GX), lax.axis_index("gy"), n_gx, n_gy, lax.axis_index(CORE)]
    ).astype(jnp.int32)

    out_up, out_down, out_mid, gcol = call_pick(place, ghost_count, ghost_rows, nodes)
    up = lax.ppermute(out_up, GX, ring(n_gx, 1))
    down = lax.ppermute(out_down, GX, ring(n_gx, -1))
    recvs, rcol = call_own(edge_count, edge_recv, nodes)
    up, down, recvs = lax.optimization_barrier((up, down, recvs))

    yup = lax.ppermute(
        jnp.concatenate(
            [up[2 * slots :], out_mid[slots:], down[2 * slots :], d_coarse[coarse - BAND :]]
        ),
        "gy",
        ring(n_gy, 1),
    )
    ydown = lax.ppermute(
        jnp.concatenate([up[:slots], out_mid[:slots], down[:slots], d_coarse[:BAND]]),
        "gy",
        ring(n_gy, -1),
    )
    sown, scol = call_own(edge_count, edge_send, nodes)

    (senders, act, slope, fine_out, summed, nact, nslope, window, wlow, whigh) = call_forward(
        edge_count,
        edge_recv,
        coarse + 2 * BAND,
        scol,
        rcol,
        sown,
        recvs,
        up,
        down,
        yup,
        ydown,
        nodes,
        pool_map,
        w_edge_in,
        w_edge_out,
        w_node_in,
        w_node_out,
    )

    nlow = lax.ppermute(whigh, "gy", ring(n_gy, 1))
    nhigh = lax.ppermute(wlow, "gy", ring(n_gy, -1))

    coarse_out, d_node, d_edge, keep, give = call_backward(
        place,
        (rcol, senders, recvs, act, slope),
        (
            window,
            nlow,
            nhigh,
            yup[3 * slots :],
            ydown[3 * slots :],
            d_coarse,
            d_fine,
            pool_map,
            nodes,
            summed,
            nact,
            nslope,
            w_edge_in,
            w_edge_out,
            w_node_in,
            w_node_out,
            w_coarse_in,
            w_coarse_out,
        ),
    )
    swap = ring(lax.axis_size(CORE), 1)
    got = lax.ppermute(give, CORE, swap)
    own = scattered((keep.astype(f32) + got.astype(f32)).astype(bf16))
    r_down, r_up, r_own = call_ghost(edge_count, edge_send, d_edge, w_edge_in, owned, slots)
    own, r_down, r_up, r_own = lax.optimization_barrier((own, r_down, r_up, r_own))
    high = lax.ppermute(r_down, "gy", ring(n_gy, -1))
    low = lax.ppermute(r_up, "gy", ring(n_gy, 1))
    own = to_all(own, "gy").astype(f32).sum(axis=0).astype(bf16)
    d_own = call_local(edge_count, edge_send, edge_recv, d_edge, d_node, w_edge_in)
    ret_up = lax.ppermute(
        jnp.concatenate([low[:slots], r_own[slots:], high[:slots]]), GX, ring(n_gx, -1)
    )
    ret_down = lax.ppermute(
        jnp.concatenate([low[2 * slots :], r_own[:slots], high[2 * slots :]]), GX, ring(n_gx, 1)
    )
    own, ret_down, ret_up, d_own = lax.optimization_barrier((own, ret_down, ret_up, d_own))
    half = to_all(own, CHIPS).reshape(keep.shape)
    grad_nodes = call_return(
        place, ghost_count, ghost_rows, gcol, ret_down, ret_up, low, high, d_own
    )
    half, grad_nodes = lax.optimization_barrier((half, grad_nodes))
    other = lax.ppermute(half, CORE, swap)
    scaled = call_scale(1.0 / (owned * n_gx * n_gy) ** 0.5, place, half, other)
    return (fine_out, coarse_out, grad_nodes, *scaled)


def solution(mesh):
    torus = Mesh(mesh.devices.reshape(4, 4, 2, mesh.shape["gy"]), GX_GY)
    in_specs = (
        P(GX_GY, None),
        P(GX_GY, None, None),
        P(GX_GY, None),
        P(GX_GY, None),
        P(GX_GY, None),
        P(GX_GY),
        P(GX_GY, None),
        P(),
        P(),
        P(),
        P(),
        P(),
        P(),
        P(GX_GY, None),
        P(GX_GY, None),
    )
    out_specs = (P(GX_GY, None), P(GX_GY, None), P(GX_GY, None), P(), P(), P(), P(), P(), P())
    return jax.shard_map(body, mesh=torus, in_specs=in_specs, out_specs=out_specs, check_vma=False)
```
